256 devices in a mesh: gx: 4 (over y_lo, core), gy: 8 (over z), gz: 8 (over x, y_hi).
Axes of the slice: x: 4, y: 4 (y_hi: 2, y_lo: 2; y = y_hi * 2 + y_lo), z: 8, core: 2. Of those that a mesh axis runs over, the one named last changes fastest.
Arguments:
- design: float32 [64, 256, 1024], P('gx', 'gy', 'gz'), may hold values from 0 to 1
- modes: float32 [2, 3, 64, 256, 1024], P(None, None, 'gx', 'gy', 'gz'), may hold values from -14 to 14
- eigenvalues: float32 [2], replicated, may hold values from 4 to 40
Outputs:
- sensitivity: float32 [2, 64, 256, 1024], P(None, 'gx', 'gy', 'gz')
The draws below stay inside these ranges and needn't reach their ends.
All inputs are finite; a program needn't handle non-finite values.
Results may differ from the reference program's by a relative error of at most 0.0001.
Values sent between devices are 32-bit elements; how exact they have to be, the bound alone decides.
A program may use at most 128 MiB of HBM per device.

```python
import math
import jax
import jax.numpy as jnp
import numpy as np
from jax import lax

MODES = 2
NX = 64
NY = 256
NZ = 1024


def draw_modes(key, part):
    key = jax.random.fold_in(key, 11)
    shape = (MODES, 3, NX, NY, NZ)
    base = jnp.clip(jax.random.normal(key, shape, jnp.float32), -4.0, 4.0)
    along_x = jnp.arange(NX, dtype=jnp.float32)[:, None, None] / NX
    along_y = jnp.arange(NY, dtype=jnp.float32)[None, :, None] / NY
    along_z = jnp.arange(NZ, dtype=jnp.float32)[None, None, :] / NZ
    ramp = 0.5 + along_x + along_y + along_z
    return base * ramp[None, None]


def block_scale(own_key, dims, split, low, top_value):
    def one(axis_at, shards_of):
        heights = jax.random.uniform(jax.random.fold_in(jax.random.fold_in(own_key, 6), axis_at), (shards_of,), jnp.float32, low / len(split), top_value / len(split))
        return jnp.repeat(jnp.exp(heights), dims[axis_at] // shards_of).reshape((-1,) + (1,) * (len(dims) - axis_at - 1))

    gain = one(*split[0])
    for cut in split[1:]:
        gain = gain * one(*cut)
    return gain


def setup_inputs(seed: int = 0) -> dict:
    splits = jax.random.split(jax.random.key(seed), 4)
    design = jnp.clip(1.0 * jax.random.uniform(splits[0], (NX, NY, NZ), jnp.float32) ** block_scale(splits[0], (NX, NY, NZ), ((0, 4), (1, 8), (2, 8)), -0.2, 0.2), 0.0, 1.0)
    modes = draw_modes(jax.random.fold_in(splits[3], 71), 0)
    eigenvalues = jnp.clip(jnp.exp(jax.random.uniform(splits[2], (MODES,), jnp.float32, math.log(4.0), math.log(40.0))), 4.0, 40.0)
    return {"design": design, "modes": modes, "eigenvalues": eigenvalues}


def offset_table():
    table = []
    for ox in range(-2, 3):
        for oy in range(-2, 3):
            for oz in range(-2, 3):
                radius = math.sqrt(ox * ox + oy * oy + oz * oz)
                if radius < 3.0:
                    table.append((ox, oy, oz, 3.0 - radius))
    return table

def element_tables():
    points = [(1.0 - 1.0 / math.sqrt(3.0)) / 2.0, (1.0 + 1.0 / math.sqrt(3.0)) / 2.0]
    poisson = 0.3
    factor = 1.0 / ((1.0 + poisson) * (1.0 - 2.0 * poisson))
    elastic = np.zeros((6, 6))
    elastic[:3, :3] = poisson * factor
    for i in range(3):
        elastic[i, i] = (1.0 - poisson) * factor
        elastic[3 + i, 3 + i] = (1.0 - 2.0 * poisson) / 2.0 * factor
    stiff = np.zeros((24, 24))
    mass = np.zeros((24, 24))
    for px in points:
        for py in points:
            for pz in points:
                shapes = np.zeros(8)
                grads = np.zeros((8, 3))
                for a in range(2):
                    for b in range(2):
                        for c in range(2):
                            node = 4 * a + 2 * b + c
                            fx = px if a else 1.0 - px
                            fy = py if b else 1.0 - py
                            fz = pz if c else 1.0 - pz
                            dx = 1.0 if a else -1.0
                            dy = 1.0 if b else -1.0
                            dz = 1.0 if c else -1.0
                            shapes[node] = fx * fy * fz
                            grads[node] = [dx * fy * fz, fx * dy * fz, fx * fy * dz]
                strain = np.zeros((6, 24))
                for node in range(8):
                    gxv, gyv, gzv = grads[node]
                    col = 3 * node
                    strain[0, col] = gxv
                    strain[1, col + 1] = gyv
                    strain[2, col + 2] = gzv
                    strain[3, col] = gyv
                    strain[3, col + 1] = gxv
                    strain[4, col + 1] = gzv
                    strain[4, col + 2] = gyv
                    strain[5, col] = gzv
                    strain[5, col + 2] = gxv
                stiff += 0.125 * strain.T @ elastic @ strain
                mass += 0.125 * np.kron(np.outer(shapes, shapes), np.eye(3))
    return np.concatenate([stiff, mass], axis=0).astype(np.float32)

def apply_filter(padded, shape):
    total = None
    for ox, oy, oz, weight in offset_table():
        piece = padded[..., 2 + ox:2 + ox + shape[0], 2 + oy:2 + oy + shape[1], 2 + oz:2 + oz + shape[2]]
        total = weight * piece if total is None else total + weight * piece
    return total

def element_terms(nodes, shape):
    table = jnp.asarray(element_tables()).astype(nodes.dtype)
    slabs = shape[0] // 4

    def slab(start):
        piece = lax.dynamic_slice_in_dim(nodes, start, 5, 2)
        corners = []
        for a in range(2):
            for b in range(2):
                for c in range(2):
                    corners.append(piece[:, :, a:a + 4, b:b + shape[1], c:c + shape[2]])
        stacked = jnp.stack(corners, axis=1)
        vectors = stacked.reshape(stacked.shape[0], 24, 4, shape[1], shape[2])
        images = jnp.einsum('pq,mqxyz->mpxyz', table, vectors, precision=lax.Precision.HIGHEST)
        stiff_term = lax.optimization_barrier(jnp.sum(vectors * images[:, :24], axis=1))
        mass_term = lax.optimization_barrier(jnp.sum(vectors * images[:, 24:], axis=1))
        return (stiff_term, mass_term)
    starts = jnp.arange(slabs, dtype=jnp.int32) * 4
    stiff_all, mass_all = lax.map(slab, starts)

    def order(values):
        moved = jnp.moveaxis(values, 0, 1)
        return moved.reshape(moved.shape[0], shape[0], shape[1], shape[2])
    return (order(stiff_all), order(mass_all))

def project(filtered):
    rise = jnp.tanh(8.0 * (filtered - 0.5))
    scale = 2.0 * jnp.tanh(jnp.asarray(4.0, filtered.dtype))
    physical = (jnp.tanh(jnp.asarray(4.0, filtered.dtype)) + rise) / scale
    slope = 8.0 * (1.0 - rise * rise) / scale
    return (physical, slope)

def reference(design, modes, eigenvalues):
    shape = design.shape
    ones = jnp.ones(shape, design.dtype)
    weight_sum = apply_filter(jnp.pad(ones, 2), shape)
    filtered = apply_filter(jnp.pad(design, 2), shape) / weight_sum
    physical, slope = project(filtered)
    nodes = jnp.pad(modes, ((0, 0), (0, 0), (0, 1), (0, 1), (0, 1)))
    stiff_term, mass_term = element_terms(nodes, shape)
    mass_total = lax.optimization_barrier(jnp.sum(physical[None] * mass_term, axis=(1, 2, 3)))
    grad = 3.0 * (1.0 - 0.001) * physical[None] ** 2 * stiff_term - eigenvalues[:, None, None, None] * mass_term
    grad = grad * (slope / weight_sum)[None] / mass_total[:, None, None, None]
    padded = jnp.pad(grad, ((0, 0), (2, 2), (2, 2), (2, 2)))
    return apply_filter(padded, shape) * float(NX * NY * NZ)
```

```python
import itertools
import math

import jax
import jax.numpy as jnp
from jax import lax
from jax.experimental import pallas as pl
from jax.experimental.pallas import tpu as pltpu
from jax.sharding import PartitionSpec as P

AXES = ("gx", "gy", "gz")
MESH = pl.DeviceIdType.MESH
TX, TY, TZ = 16, 32, 128
NEAR = [o for o in itertools.product((-1, 0, 1), repeat=3) if o != (0, 0, 0)]
FLAT = [o for o in NEAR if o[2] == 0]
F32 = jnp.float32


def weight(i, j, k):
    return max(0.0, 3.0 - math.sqrt(i * i + j * j + k * k))


def column(dx, dy):
    return (dx + 1) * 3 + (dy + 1)


X_SPAN = {-1: (0, TX + 2, 2), 0: (0, 2, TX), 1: (TX - 2, 0, 2)}
Y_SPAN = {-1: (0, TY + 8, 2), 0: (0, 8, TY), 1: (TY - 2, 6, 2)}


def combine(a, weights):
    total = None
    for value, w in zip(a, weights):
        if w == 0.0:
            continue
        total = w * value if total is None else total + w * value
    return total


def kernel(
    sizes,
    design_ref,
    modes_ref,
    eig_ref,
    raw_ref,
    total_ref,
    dp,
    mb,
    mz,
    zl,
    zh,
    from_hi,
    from_lo,
    sz,
    phys,
    slope,
    gp,
    gl,
    gh,
    g_from_hi,
    g_from_lo,
    outs,
    a_in,
    b_in,
    local_sem,
    out_sem,
    d_send,
    d_recv,
    m_send,
    m_recv,
    g_send,
    g_recv,
    a_send,
    a_recv,
    b_send,
    b_recv,
):
    cx, cy, cz = sizes
    me = tuple(lax.axis_index(a) for a in AXES)
    mx, my, mzi = me

    def near(o):
        return tuple(lax.rem(m + (d + s), s) for m, d, s in zip(me, o, sizes))

    a_count, b_count = (cx // 2) * cz, 2 * cy
    a_slot = (mx // 2) * cz + mzi
    b_slot = lax.rem(mx, 2) * cy + my

    def a_device(k):
        slot = lax.rem(a_slot + k, a_count)
        return ((slot // cz) * 2 + lax.rem(mx, 2), my, lax.rem(slot, cz))

    def b_device(k):
        slot = lax.rem(b_slot + k, b_count)
        return ((mx // 2) * 2 + slot // cy, lax.rem(slot, cy), mzi)

    barrier = pltpu.get_barrier_semaphore()
    for o in NEAR:
        pl.semaphore_signal(barrier, inc=1, device_id=near(o), device_id_type=MESH)
    for k in range(1, a_count):
        pl.semaphore_signal(barrier, inc=1, device_id=a_device(k), device_id_type=MESH)
    for k in range(1, b_count):
        pl.semaphore_signal(barrier, inc=1, device_id=b_device(k), device_id_type=MESH)

    load_design = pltpu.make_async_copy(
        design_ref, dp.at[pl.ds(2, TX), pl.ds(8, TY)], local_sem.at[0]
    )
    load_design.start()
    load_modes = pltpu.make_async_copy(
        modes_ref, mb.at[:, pl.ds(0, TX), pl.ds(0, TY)], local_sem.at[1]
    )
    load_modes.start()

    lane = lax.broadcasted_iota(jnp.int32, (8, 128), 1)
    pair = lax.shift_right_logical(lane, 1)
    zero = jnp.zeros((8, 128), F32)

    load_design.wait()

    def pack_design(x, carry):
        lo, hi = carry
        for g in range(4):
            k = 4 * x + g
            r = pltpu.roll(dp[x + 2, 8 + 8 * g : 16 + 8 * g, :], 2 * k, 1)
            lo = jnp.where(pair == k, r, lo)
            hi = jnp.where(pair == lax.rem(k + 63, 64), r, hi)
        return lo, hi

    lo, hi = lax.fori_loop(0, TX, pack_design, (zero, zero))
    zl[0] = lo
    zh[0] = hi

    load_modes.wait()

    def pack_modes(x, carry):
        carry = list(carry)
        for c in range(6):
            for g in range(4):
                k = (c % 2) * 64 + 4 * x + g
                r = pltpu.roll(mb[c, x, 8 * g : 8 * g + 8, :], k, 1)
                carry[c // 2] = jnp.where(lane == k, r, carry[c // 2])
        return tuple(carry)

    packed = lax.fori_loop(0, TX, pack_modes, (zero, zero, zero))
    for i in range(3):
        zl[1 + i] = packed[i]

    pl.semaphore_wait(barrier, len(NEAR) + a_count - 1 + b_count - 1)

    d_copies, m_copies = [], []

    def send(o, src, dst, copies, send_sems, recv_sems):
        i = len(copies)
        copy = pltpu.make_async_remote_copy(
            src_ref=src,
            dst_ref=dst,
            send_sem=send_sems.at[i],
            recv_sem=recv_sems.at[i],
            device_id=near(o),
            device_id_type=MESH,
        )
        copy.start()
        copies.append(copy)

    for o in NEAR:
        dx, dy, dz = o
        if dz == 0:
            (xs, xd, xn), (ys, yd, yn) = X_SPAN[dx], Y_SPAN[dy]
            src = design_ref.at[pl.ds(xs, xn), pl.ds(ys, yn)]
            dst = dp.at[pl.ds(xd, xn), pl.ds(yd, yn)]
        elif dz == 1:
            src, dst = zh, from_lo.at[column(-dx, -dy)]
        elif dx <= 0 and dy <= 0:
            src, dst = zl, from_hi.at[column(-dx, -dy)]
        else:
            src = zl.at[pl.ds(0, 1)]
            dst = from_hi.at[column(-dx, -dy), pl.ds(0, 1)]
        send(o, src, dst, d_copies, d_send, d_recv)
    for o in ((-1, 0, 0), (0, -1, 0), (-1, -1, 0)):
        dx, dy, _ = o
        xs = pl.ds(0, 1) if dx else pl.ds(0, TX)
        xd = pl.ds(TX, 1) if dx else pl.ds(0, TX)
        ys = pl.ds(0, 1) if dy else pl.ds(0, TY)
        yd = pl.ds(TY, 1) if dy else pl.ds(0, TY)
        send(o, modes_ref.at[:, xs, ys], mb.at[:, xd, yd], m_copies, m_send, m_recv)

    def inside(cell, total):
        return ((cell >= 0) & (cell < total)).astype(F32)

    zpos = mzi * TZ + lax.broadcasted_iota(jnp.int32, (8, 128), 1)
    z1 = inside(zpos - 1, cz * TZ) + inside(zpos + 1, cz * TZ)
    z2 = inside(zpos - 2, cz * TZ) + inside(zpos + 2, cz * TZ)
    parts = []
    for g in range(4):
        ypos = my * TY + 8 * g + lax.broadcasted_iota(jnp.int32, (8, 128), 0)
        y1 = inside(ypos - 1, cy * TY) + inside(ypos + 1, cy * TY)
        y2 = inside(ypos - 2, cy * TY) + inside(ypos + 2, cy * TY)
        row = []
        for i in range(3):
            rows = [
                weight(i, j, 0) + weight(i, j, 1) * z1 + weight(i, j, 2) * z2 for j in range(3)
            ]
            row.append(rows[0] + y1 * rows[1] + y2 * rows[2])
        parts.append(row)

    x_lo = (mx > 0).astype(F32)
    x_hi = (mx < cx - 1).astype(F32)
    y_lo = (my > 0).astype(F32)
    y_hi = (my < cy - 1).astype(F32)
    z_lo = (mzi > 0).astype(F32)
    z_hi = (mzi < cz - 1).astype(F32)

    def clear_halo(ref, lead):
        @pl.when(mx == 0)
        def _():
            ref[lead + (slice(0, 2),)] = jnp.zeros_like(ref[lead + (slice(0, 2),)])

        @pl.when(mx == cx - 1)
        def _():
            ref[lead + (slice(TX + 2, TX + 4),)] = jnp.zeros_like(
                ref[lead + (slice(TX + 2, TX + 4),)]
            )

        @pl.when(my == 0)
        def _():
            ref[lead + (slice(None), slice(0, 8))] = jnp.zeros_like(
                ref[lead + (slice(None), slice(0, 8))]
            )

        @pl.when(my == cy - 1)
        def _():
            ref[lead + (slice(None), slice(TY + 8, TY + 16))] = jnp.zeros_like(
                ref[lead + (slice(None), slice(TY + 8, TY + 16))]
            )

    def spread(load, hi_of, lo_of):
        def body(p, _):
            cxi = (p + 14) // 16
            xs = lax.rem(p + 14, 16)
            xmask = jnp.where(cxi == 0, x_lo, jnp.where(cxi == 2, x_hi, 1.0))
            for g in range(6):
                cyi = 0 if g == 0 else 2 if g == 5 else 1
                ys = 3 if g == 0 else 0 if g == 5 else g - 1
                mask = xmask * (y_lo if g == 0 else y_hi if g == 5 else 1.0)
                k = 4 * xs + ys
                back = lax.rem(128 - 2 * k, 128)
                n = cxi * 3 + cyi
                v = load(p, g)
                h_hi = pltpu.roll(hi_of(n), back, 1) * (mask * z_hi)
                h_lo = pltpu.roll(lo_of(n), back, 1) * (mask * z_lo)
                up = jnp.where(lane < 1, h_hi, v)
                down = jnp.where(lane >= 127, h_lo, v)
                up2 = jnp.where(lane < 2, h_hi, v)
                down2 = jnp.where(lane >= 126, h_lo, v)
                rows = slice(8 * g, 8 * g + 8)
                sz[0, p, rows, :] = pltpu.roll(up, 127, 1) + pltpu.roll(down, 1, 1)
                sz[1, p, rows, :] = pltpu.roll(up2, 126, 1) + pltpu.roll(down2, 2, 1)
            return 0

        lax.fori_loop(0, TX + 4, body, 0)

    order = ((0, 0), (0, 1), (1, 1), (0, 2), (1, 2), (2, 2))

    def filtered(load, store):
        def body(p, carry):
            new = []
            for g in range(4):
                terms = {}
                for k in range(3):
                    ref = load if k == 0 else (lambda q, a, b, k=k: sz[k - 1, q, a:b, :])
                    top = 8 + 8 * g
                    terms[0, k] = ref(p, top, top + 8)
                    terms[1, k] = ref(p, top - 1, top + 7) + ref(p, top + 1, top + 9)
                    terms[2, k] = ref(p, top - 2, top + 6) + ref(p, top + 2, top + 10)
                grouped = [
                    terms[i, j] if i == j else terms[i, j] + terms[j, i] for i, j in order
                ]
                f = [
                    combine(grouped, [weight(i, j, k) for j, k in order]) for i in range(3)
                ]
                a0, a1, a2, a3 = carry[4 * g : 4 * g + 4]
                store(p, g, a0 + f[2])
                new += [a1 + f[1], a2 + f[0], a3 + f[1], f[2]]
            return tuple(new)

        lax.fori_loop(0, TX + 4, body, (zero,) * 16)

    for copy in d_copies:
        copy.wait_recv()
    clear_halo(dp, ())
    spread(
        lambda p, g: dp[p, 8 * g : 8 * g + 8, :],
        lambda n: from_hi[n, 0],
        lambda n: from_lo[n, 0],
    )

    top_t = math.tanh(4.0)

    def project(p, g, value):
        xpos = mx * TX + p - 4
        x1 = inside(xpos - 1, cx * TX) + inside(xpos + 1, cx * TX)
        x2 = inside(xpos - 2, cx * TX) + inside(xpos + 2, cx * TX)
        inverse = 1.0 / (parts[g][0] + x1 * parts[g][1] + x2 * parts[g][2])
        t = jnp.tanh(8.0 * (value * inverse - 0.5))
        rows = slice(8 * g, 8 * g + 8)
        phys[p, rows, :] = (top_t + t) * (0.5 / top_t)
        slope[p, rows, :] = (1.0 - t * t) * inverse * (4.0 / top_t)

    filtered(lambda p, a, b: dp[p, a:b, :], project)

    for copy in m_copies:
        copy.wait_recv()

    @pl.when(mx == cx - 1)
    def _():
        mb[:, TX] = jnp.zeros_like(mb[:, TX])

    @pl.when(my == cy - 1)
    def _():
        mb[:, :, TY : TY + 8] = jnp.zeros_like(mb[:, :, TY : TY + 8])

    def shift_modes(x, _):
        cxi = x // 16
        xs = lax.rem(x, 16)
        xmask = jnp.where(cxi == 1, x_hi, 1.0) * z_hi
        for c in range(6):
            for g in range(5):
                ys = g % 4
                k = (c % 2) * 64 + 4 * xs + ys
                n = (cxi + 1) * 3 + 1 + g // 4
                mask = xmask * (y_hi if g == 4 else 1.0)
                h = pltpu.roll(from_hi[n, 1 + c // 2], lax.rem(128 - k, 128), 1) * mask
                v = jnp.where(lane == 0, h, mb[c, x, 8 * g : 8 * g + 8, :])
                mz[c, x, 8 * g : 8 * g + 8, :] = pltpu.roll(v, 127, 1)
        return 0

    lax.fori_loop(0, TX + 1, shift_modes, 0)

    factor = 1.0 / (1.3 * 0.4)
    lam, mu = 0.3 * factor, 0.2 * factor

    def plane(c, x, g):
        a, b = 8 * g, 8 * g + 8
        v0, v1 = mb[c, x, a:b, :], mb[c, x, a + 1 : b + 1, :]
        w0, w1 = mz[c, x, a:b, :], mz[c, x, a + 1 : b + 1, :]
        vs, vd, ws, wd = v0 + v1, v1 - v0, w0 + w1, w1 - w0
        return vs + ws, ws - vs, vd + wd, wd - vd

    def energies(now, later):
        a = {}
        for c in range(3):
            for q, (j, k) in enumerate(((0, 0), (0, 1), (1, 0), (1, 1))):
                a[c, 0, j, k] = now[4 * c + q] + later[4 * c + q]
                a[c, 1, j, k] = later[4 * c + q] - now[4 * c + q]
        s = {key: v * v for key, v in a.items()}

        def sq(v):
            return v * v

        q0 = s[0, 0, 0, 0] + s[1, 0, 0, 0] + s[2, 0, 0, 0]
        axial = s[0, 1, 0, 0] + s[1, 0, 1, 0] + s[2, 0, 0, 1]
        q1 = axial + (
            (s[0, 0, 1, 0] + s[0, 0, 0, 1])
            + (s[1, 1, 0, 0] + s[1, 0, 0, 1])
            + (s[2, 1, 0, 0] + s[2, 0, 1, 0])
        )
        bend = (
            (s[0, 1, 1, 0] + s[0, 1, 0, 1])
            + (s[1, 1, 1, 0] + s[1, 0, 1, 1])
            + (s[2, 1, 0, 1] + s[2, 0, 1, 1])
        )
        q2 = bend + (s[0, 0, 1, 1] + s[1, 1, 0, 1] + s[2, 1, 1, 0])
        q3 = s[0, 1, 1, 1] + s[1, 1, 1, 1] + s[2, 1, 1, 1]
        mass = (1 / 64) * q0 + (1 / 192) * q1 + ((1 / 576) * q2 + (1 / 1728) * q3)
        trace = sq(a[0, 1, 0, 0] + a[1, 0, 1, 0] + a[2, 0, 0, 1])
        shear = (
            sq(a[0, 0, 1, 0] + a[1, 1, 0, 0])
            + sq(a[1, 0, 0, 1] + a[2, 0, 1, 0])
            + sq(a[0, 0, 0, 1] + a[2, 1, 0, 0])
        )
        trace_1 = (
            sq(a[0, 1, 1, 0] + a[2, 0, 1, 1])
            + sq(a[0, 1, 0, 1] + a[1, 0, 1, 1])
            + sq(a[1, 1, 1, 0] + a[2, 1, 0, 1])
        )
        shear_1 = (
            sq(a[0, 0, 1, 1] + a[1, 1, 0, 1])
            + sq(a[1, 1, 0, 1] + a[2, 1, 1, 0])
            + sq(a[0, 0, 1, 1] + a[2, 1, 1, 0])
        )
        stiff = (
            ((lam / 16) * trace + (mu / 8) * axial)
            + ((mu / 16) * shear + (lam / 48) * trace_1)
            + ((mu / 16) * bend + (mu / 48) * shear_1)
            + ((lam + 4 * mu) / 144) * q3
        )
        return stiff, mass

    packs = []
    masses = []
    for m in range(2):
        eig = eig_ref[m]
        lo, hi, acc = zero, zero, zero
        for pairs in range(2):
            groups = (2 * pairs, 2 * pairs + 1)

            def body(x, carry, m=m, groups=groups, eig=eig):
                lo, hi, acc = carry[:3]
                held = carry[3:]
                nexts = []
                for i, g in enumerate(groups):
                    now = held[12 * i : 12 * i + 12]
                    later = sum((plane(3 * m + c, x + 1, g) for c in range(3)), ())
                    nexts += later
                    stiff, mass = energies(now, later)
                    rows = slice(8 * g, 8 * g + 8)
                    rho = phys[x + 4, rows, :]
                    acc = acc + rho * mass
                    grad = ((3.0 * (1.0 - 0.001)) * (rho * rho) * stiff - eig * mass) * slope[
                        x + 4, rows, :
                    ]
                    gp[m, x + 2, 8 + 8 * g : 16 + 8 * g, :] = grad
                    k = 4 * x + g
                    r = pltpu.roll(grad, 2 * k, 1)
                    lo = jnp.where(pair == k, r, lo)
                    hi = jnp.where(pair == lax.rem(k + 63, 64), r, hi)
                return (lo, hi, acc, *nexts)

            first = []
            for g in groups:
                first += sum((plane(3 * m + c, 0, g) for c in range(3)), ())
            lo, hi, acc = lax.fori_loop(0, TX, body, (lo, hi, acc, *first))[:3]
        packs.append((lo, hi))
        masses.append(acc)
    for m in range(2):
        gl[m] = packs[m][0]
        gh[m] = packs[m][1]
        a_in[0, m : m + 1, :] = jnp.sum(masses[m], axis=0, keepdims=True)

    a_copies = []
    for k in range(1, a_count):
        copy = pltpu.make_async_remote_copy(
            src_ref=a_in.at[0],
            dst_ref=a_in.at[k],
            send_sem=a_send.at[k],
            recv_sem=a_recv.at[k],
            device_id=a_device(k),
            device_id_type=MESH,
        )
        copy.start()
        a_copies.append(copy)

    g_copies = []
    for o in NEAR:
        dx, dy, dz = o
        if dz == 0:
            (xs, xd, xn), (ys, yd, yn) = X_SPAN[dx], Y_SPAN[dy]
            src = gp.at[:, pl.ds(xs + 2, xn), pl.ds(ys + 8, yn)]
            dst = gp.at[:, pl.ds(xd, xn), pl.ds(yd, yn)]
        elif dz == 1:
            src, dst = gh, g_from_lo.at[column(-dx, -dy)]
        else:
            src, dst = gl, g_from_hi.at[column(-dx, -dy)]
        send(o, src, dst, g_copies, g_send, g_recv)

    for copy in a_copies:
        copy.wait_recv()
    b_in[0] = jnp.sum(a_in[...], axis=0)
    b_copies = []
    for k in range(1, b_count):
        copy = pltpu.make_async_remote_copy(
            src_ref=b_in.at[0],
            dst_ref=b_in.at[k],
            send_sem=b_send.at[k],
            recv_sem=b_recv.at[k],
            device_id=b_device(k),
            device_id_type=MESH,
        )
        copy.start()
        b_copies.append(copy)

    for copy in g_copies:
        copy.wait_recv()
    clear_halo(gp, (slice(None),))
    stores = []
    for m in range(2):
        spread(
            lambda p, g, m=m: gp[m, p, 8 * g : 8 * g + 8, :],
            lambda n, m=m: g_from_hi[n, m],
            lambda n, m=m: g_from_lo[n, m],
        )

        def keep(p, g, value, m=m):
            outs[m, p, 8 * g : 8 * g + 8, :] = value

        filtered(lambda p, a, b, m=m: gp[m, p, a:b, :], keep)
        store = pltpu.make_async_copy(
            outs.at[m, pl.ds(4, TX)], raw_ref.at[m], out_sem.at[m]
        )
        store.start()
        stores.append(store)

    for copy in b_copies:
        copy.wait_recv()
    total = jnp.sum(jnp.sum(b_in[...], axis=0), axis=1, keepdims=True)
    total_ref[...] = jnp.broadcast_to(total, (2, 128))

    for copy in d_copies + m_copies + a_copies + g_copies + b_copies:
        copy.wait_send()
    for store in stores:
        store.wait()


def per_device(sizes, design, modes, eigenvalues):
    cx, cy, cz = sizes
    a_count, b_count = (cx // 2) * cz, 2 * cy
    count = float(cx * TX * cy * TY * cz * TZ)
    dma = pltpu.SemaphoreType.DMA

    def vmem(*shape):
        return pltpu.VMEM(shape, F32)

    raw, total = pl.pallas_call(
        lambda *refs: kernel(sizes, *refs),
        out_shape=(
            jax.ShapeDtypeStruct((2, TX, TY, TZ), F32),
            jax.ShapeDtypeStruct((2, 128), F32),
        ),
        in_specs=[
            pl.BlockSpec(memory_space=pl.ANY),
            pl.BlockSpec(memory_space=pl.ANY),
            pl.BlockSpec(memory_space=pltpu.SMEM),
        ],
        out_specs=(
            pl.BlockSpec(memory_space=pl.ANY),
            pl.BlockSpec(memory_space=pltpu.VMEM),
        ),
        scratch_shapes=[
            vmem(TX + 4, TY + 16, TZ),
            vmem(6, TX + 1, TY + 8, TZ),
            vmem(6, TX + 1, TY + 8, TZ),
            vmem(4, 8, 128),
            vmem(1, 8, 128),
            vmem(9, 4, 8, 128),
            vmem(9, 1, 8, 128),
            vmem(2, TX + 4, TY + 16, TZ),
            vmem(TX + 4, TY, TZ),
            vmem(TX + 4, TY, TZ),
            vmem(2, TX + 4, TY + 16, TZ),
            vmem(2, 8, 128),
            vmem(2, 8, 128),
            vmem(9, 2, 8, 128),
            vmem(9, 2, 8, 128),
            vmem(2, TX + 4, TY, TZ),
            vmem(a_count, 2, 128),
            vmem(b_count, 2, 128),
            dma((2,)),
            dma((2,)),
            dma((26,)),
            dma((26,)),
            dma((3,)),
            dma((3,)),
            dma((26,)),
            dma((26,)),
            dma((a_count,)),
            dma((a_count,)),
            dma((b_count,)),
            dma((b_count,)),
        ],
        compiler_params=pltpu.CompilerParams(
            collective_id=0, has_side_effects=True, vmem_limit_bytes=40 * 1024 * 1024
        ),
    )(design, modes.reshape(6, TX, TY, TZ), eigenvalues)
    return raw * (count / total[:, 0])[:, None, None, None]


def solution(mesh):
    sizes = tuple(mesh.shape[a] for a in AXES)
    return jax.shard_map(
        lambda design, modes, eigenvalues: per_device(sizes, design, modes, eigenvalues),
        mesh=mesh,
        in_specs=(P("gx", "gy", "gz"), P(None, None, "gx", "gy", "gz"), P()),
        out_specs=P(None, "gx", "gy", "gz"),
        check_vma=False,
    )
```

```python
import itertools
import math

import jax
import jax.numpy as jnp
from jax import lax
from jax.experimental import pallas as pl
from jax.experimental.pallas import tpu as pltpu
from jax.sharding import PartitionSpec as P

AXES = ("gx", "gy", "gz")
MESH = pl.DeviceIdType.MESH
TX, TY, TZ = 16, 32, 128
FLAT = [o for o in itertools.product((-1, 0, 1), (-1, 0, 1), (0,)) if o != (0, 0, 0)]
BELOW = [(0, 0, -1), (0, -1, -1), (-1, 0, -1), (-1, -1, -1)]
F32 = jnp.float32


def weight(i, j, k):
    return max(0.0, 3.0 - math.sqrt(i * i + j * j + k * k))


X_SPAN = {-1: (0, TX + 2, 2), 0: (0, 2, TX), 1: (TX - 2, 0, 2)}
Y_SPAN = {-1: (0, TY + 8, 2), 0: (0, 8, TY), 1: (TY - 2, 6, 2)}


def combine(values, weights):
    total = None
    for value, w in zip(values, weights):
        if w == 0.0:
            continue
        total = w * value if total is None else total + w * value
    return total


def loop(n, body, init, by=1):
    def block(q, carry):
        for i in range(by):
            carry = body(q * by + i, carry)
        return carry

    return block(0, init) if by == n else lax.fori_loop(0, n // by, block, init)


def kernel(
    sizes,
    design_ref,
    modes_ref,
    eig_ref,
    raw_ref,
    total_ref,
    dp,
    mb,
    mz,
    face,
    from_hi,
    wparts,
    fz,
    stiffs,
    mass_terms,
    gp,
    outs,
    z_out,
    z_up,
    z_down,
    a_in,
    b_in,
    eig,
    local_sem,
    out_sem,
    send_sem,
    recv_sem,
):
    cx, cy, cz = sizes
    me = tuple(lax.axis_index(a) for a in AXES)
    mx, my, mzi = me

    def near(o):
        return tuple(
            m if d == 0 else lax.rem(m + (d + s), s) for m, d, s in zip(me, o, sizes)
        )

    a_count, b_count = (cx // 2) * cz, 2 * cy
    a_slot = (mx // 2) * cz + mzi
    b_slot = lax.rem(mx, 2) * cy + my

    def a_device(k):
        slot = lax.rem(a_slot + k, a_count)
        return ((slot // cz) * 2 + lax.rem(mx, 2), my, lax.rem(slot, cz))

    def b_device(k):
        slot = lax.rem(b_slot + k, b_count)
        return ((mx // 2) * 2 + slot // cy, lax.rem(slot, cy), mzi)

    barrier = pltpu.get_barrier_semaphore()

    def greet(device):
        pl.semaphore_signal(barrier, inc=1, device_id=device, device_id_type=MESH)

    for o in FLAT + [(0, 0, 1)] + [tuple(-d for d in o) for o in BELOW[1:]] + [(0, 0, -1)]:
        greet(near(o))

    loads = [
        pltpu.make_async_copy(design_ref, dp.at[pl.ds(2, TX), pl.ds(8, TY)], local_sem.at[0])
    ]
    for c in range(6):
        loads.append(
            pltpu.make_async_copy(
                modes_ref.at[c], mb.at[c, pl.ds(0, TX), pl.ds(0, TY)], local_sem.at[1 + c]
            )
        )
    loads.append(pltpu.make_async_copy(eig_ref, eig, local_sem.at[7]))
    for load in loads:
        load.start()

    def greet_a(k, _):
        greet(a_device(k))
        return 0

    def greet_b(k, _):
        greet(b_device(k))
        return 0

    lax.fori_loop(1, a_count, greet_a, 0)
    lax.fori_loop(1, b_count, greet_b, 0)

    lane = lax.broadcasted_iota(jnp.int32, (8, 128), 1)
    quad = lax.shift_right_logical(lax.rem(lane + 2, 128), 2)
    first_two, last_two = lane < 2, lane >= 126
    zero = jnp.zeros((8, 128), F32)

    for load in loads:
        load.wait()

    def pack_modes(x, carry):
        carry = list(carry)
        for c in range(6):
            for g in range(4):
                k = (c % 2) * 64 + 4 * x + g
                r = pltpu.roll(mb[c, x, 8 * g : 8 * g + 8, :], k, 1)
                carry[c // 2] = jnp.where(lane == k, r, carry[c // 2])
        return tuple(carry)

    packed = loop(TX, pack_modes, (zero, zero, zero), TX)
    for i in range(3):
        face[i] = packed[i]

    pl.semaphore_wait(barrier, len(FLAT) + 2 + 3 + a_count - 1 + b_count - 1)

    sent = []

    def send(o, src, dst, sem):
        pltpu.make_async_remote_copy(
            src_ref=src,
            dst_ref=dst,
            send_sem=send_sem.at[sem],
            recv_sem=recv_sem.at[sem],
            device_id=near(o),
            device_id_type=MESH,
        ).start()

    def all_of(ref, sem):
        return pltpu.make_async_remote_copy(
            src_ref=ref,
            dst_ref=ref,
            send_sem=send_sem.at[sem],
            recv_sem=recv_sem.at[sem],
            device_id=near((0, 0, 1)),
            device_id_type=MESH,
        )

    for o in FLAT:
        (xs, xd, xn), (ys, yd, yn) = X_SPAN[o[0]], Y_SPAN[o[1]]
        send(
            o,
            design_ref.at[pl.ds(xs, xn), pl.ds(ys, yn)],
            dp.at[pl.ds(xd, xn), pl.ds(yd, yn)],
            0,
        )
    sent.append(all_of(dp.at[pl.ds(0, 13), pl.ds(0, 16)], 0))
    for o in ((-1, 0, 0), (0, -1, 0), (-1, -1, 0)):
        dx, dy, _ = o
        xs = pl.ds(0, 1) if dx else pl.ds(0, TX)
        xd = pl.ds(TX, 1) if dx else pl.ds(0, TX)
        ys = pl.ds(0, 1) if dy else pl.ds(0, TY)
        yd = pl.ds(TY, 1) if dy else pl.ds(0, TY)
        send(o, modes_ref.at[:, xs, ys], mb.at[:, xd, yd], 1)
    sent.append(all_of(mb.at[:, pl.ds(0, 7), pl.ds(0, 7)], 1))
    for o in BELOW:
        send(o, face, from_hi.at[-2 * o[0] - o[1]], 2)
    sent.append(all_of(from_hi, 2))

    def shift_modes(x, _):
        for c in range(6):
            for g in range(4):
                rows = slice(8 * g, 8 * g + 8)
                mz[c, x, rows, :] = pltpu.roll(mb[c, x, rows, :], 127, 1)
        return 0

    loop(TX, shift_modes, 0, 4)

    def inside(cell, total):
        return ((cell >= 0) & (cell < total)).astype(F32)

    zpos = mzi * TZ + lane
    z1 = inside(zpos - 1, cz * TZ) + inside(zpos + 1, cz * TZ)
    z2 = inside(zpos - 2, cz * TZ) + inside(zpos + 2, cz * TZ)
    for g in range(4):
        ypos = my * TY + 8 * g + lax.broadcasted_iota(jnp.int32, (8, 128), 0)
        y1 = inside(ypos - 1, cy * TY) + inside(ypos + 1, cy * TY)
        y2 = inside(ypos - 2, cy * TY) + inside(ypos + 2, cy * TY)
        for i in range(3):
            rows = [
                weight(i, j, 0) + weight(i, j, 1) * z1 + weight(i, j, 2) * z2 for j in range(3)
            ]
            wparts[i, g] = rows[0] + y1 * rows[1] + y2 * rows[2]

    y_hi = (my < cy - 1).astype(F32)
    x_hi = (mx < cx - 1).astype(F32)
    z_lo = (mzi > 0).astype(F32)
    z_hi = (mzi < cz - 1).astype(F32)

    def clear(ref, index, cond):
        @pl.when(cond)
        def _():
            ref[index] = jnp.zeros_like(ref[index])

    def clear_halo(ref, lead):
        clear(ref, lead + (slice(0, 2),), mx == 0)
        clear(ref, lead + (slice(TX + 2, TX + 4),), mx == cx - 1)
        clear(ref, lead + (slice(None), slice(0, 8)), my == 0)
        clear(ref, lead + (slice(None), slice(TY + 8, TY + 16)), my == cy - 1)

    order = ((0, 0), (0, 1), (1, 1), (0, 2), (1, 2), (2, 2))

    def sweep(load, put, packs):
        packs[0] = zero
        packs[1] = zero

        def body(xb, _):
            held = packs[xb // 2]
            for g in range(4):
                top = 8 + 8 * g
                a = {}
                for t in range(8):
                    p = 4 * xb + t
                    a[t, 0] = load(p, top, top + 8)
                    a[t, 1] = load(p, top - 1, top + 7) + load(p, top + 1, top + 9)
                    a[t, 2] = load(p, top - 2, top + 6) + load(p, top + 2, top + 10)
                for i in range(4):
                    b = {}
                    for j in range(3):
                        b[0, j] = a[i + 2, j]
                        b[1, j] = a[i + 1, j] + a[i + 3, j]
                        b[2, j] = a[i, j] + a[i + 4, j]
                    grouped = [b[u, v] if u == v else b[u, v] + b[v, u] for u, v in order]
                    e0, e1, e2 = (
                        combine(grouped, [weight(u, v, k) for u, v in order]) for k in range(3)
                    )
                    up, down = pltpu.roll(e1, 1, 1), pltpu.roll(e1, 127, 1)
                    up2, down2 = pltpu.roll(e2, 2, 1), pltpu.roll(e2, 126, 1)
                    out = jnp.where(lane < 1, up, jnp.where(lane >= 127, down, 0.0)) + jnp.where(
                        first_two, up2, jnp.where(last_two, down2, 0.0)
                    )
                    put(4 * xb + i, g, (e0 + ((up + down) + (up2 + down2))) - out)
                    k = lax.rem(xb, 2) * 16 + 4 * i + g
                    held = jnp.where(quad == k, pltpu.roll(out, 4 * k, 1), held)
            packs[xb // 2] = held
            return 0

        lax.fori_loop(0, 4, body, 0)

    def send_z(f):
        send((0, 0, -1), z_out.at[f], z_up.at[f], 3 + f)
        send((0, 0, 1), z_out.at[f], z_down.at[f], 6 + f)

    def merge_z(f):
        for s, ref in ((3 + f, z_up), (6 + f, z_down)):
            copy = all_of(ref.at[f], s)
            copy.wait_recv()
            sent.append(copy)
        for h in range(2):
            z_up[f, h] = jnp.where(lax.rem(lane, 4) >= 2, z_up[f, h] * z_hi, z_down[f, h] * z_lo)

    def from_z(f, xb, i, g):
        k = lax.rem(xb, 2) * 16 + 4 * i + g
        r = pltpu.roll(z_up[f, xb // 2], lax.rem(128 - 4 * k, 128), 1)
        return jnp.where(first_two | last_two, r, 0.0)

    sent[0].wait_recv()
    clear_halo(dp, ())

    def put_design(x, g, value):
        fz[x, 8 * g : 8 * g + 8, :] = value

    sweep(lambda p, a, b: dp[p, a:b, :], put_design, z_out.at[0])
    send_z(0)

    sent[1].wait_recv()
    sent[2].wait_recv()
    clear(mb, (slice(None), TX), mx == cx - 1)
    clear(mb, (slice(None), slice(None), slice(TY, TY + 8)), my == cy - 1)
    last = lane >= 127

    def patch_modes(x, _):
        for c in range(6):
            for g in range(5):
                k = (c % 2) * 64 + 4 * x + g % 4
                rows = slice(8 * g, 8 * g + 8)
                h = pltpu.roll(from_hi[g // 4, c // 2], lax.rem(255 - k, 128), 1)
                h = h * (z_hi * y_hi if g == 4 else z_hi)
                own = pltpu.roll(mb[c, x, rows, :], 127, 1) if g == 4 else mz[c, x, rows, :]
                mz[c, x, rows, :] = jnp.where(last, h, own)
        return 0

    loop(TX, patch_modes, 0, 2)

    def patch_end(c, _):
        for g in range(5):
            k = lax.rem(c, 2) * 64 + g % 4
            rows = slice(8 * g, 8 * g + 8)
            h = pltpu.roll(from_hi[2 + g // 4, c // 2], lax.rem(255 - k, 128), 1)
            h = h * (z_hi * x_hi * y_hi if g == 4 else z_hi * x_hi)
            mz[c, TX, rows, :] = jnp.where(last, h, pltpu.roll(mb[c, TX, rows, :], 127, 1))
        return 0

    loop(6, patch_end, 0, 3)

    factor = 1.0 / (1.3 * 0.4)
    lam, mu = 0.3 * factor, 0.2 * factor

    def plane(c, x, g):
        a, b = 8 * g, 8 * g + 8
        v0, v1 = mb[c, x, a:b, :], mb[c, x, a + 1 : b + 1, :]
        w0, w1 = mz[c, x, a:b, :], mz[c, x, a + 1 : b + 1, :]
        vs, vd, ws, wd = v0 + v1, v1 - v0, w0 + w1, w1 - w0
        return vs + ws, ws - vs, vd + wd, wd - vd

    def energies(now, later):
        a = {}
        for c in range(3):
            for q, (j, k) in enumerate(((0, 0), (0, 1), (1, 0), (1, 1))):
                a[c, 0, j, k] = now[4 * c + q] + later[4 * c + q]
                a[c, 1, j, k] = later[4 * c + q] - now[4 * c + q]
        s = {key: v * v for key, v in a.items()}

        def sq(v):
            return v * v

        q0 = s[0, 0, 0, 0] + s[1, 0, 0, 0] + s[2, 0, 0, 0]
        axial = s[0, 1, 0, 0] + s[1, 0, 1, 0] + s[2, 0, 0, 1]
        q1 = axial + (
            (s[0, 0, 1, 0] + s[0, 0, 0, 1])
            + (s[1, 1, 0, 0] + s[1, 0, 0, 1])
            + (s[2, 1, 0, 0] + s[2, 0, 1, 0])
        )
        bend = (
            (s[0, 1, 1, 0] + s[0, 1, 0, 1])
            + (s[1, 1, 1, 0] + s[1, 0, 1, 1])
            + (s[2, 1, 0, 1] + s[2, 0, 1, 1])
        )
        q2 = bend + (s[0, 0, 1, 1] + s[1, 1, 0, 1] + s[2, 1, 1, 0])
        q3 = s[0, 1, 1, 1] + s[1, 1, 1, 1] + s[2, 1, 1, 1]
        mass = (1 / 64) * q0 + (1 / 192) * q1 + ((1 / 576) * q2 + (1 / 1728) * q3)
        trace = sq(a[0, 1, 0, 0] + a[1, 0, 1, 0] + a[2, 0, 0, 1])
        shear = (
            sq(a[0, 0, 1, 0] + a[1, 1, 0, 0])
            + sq(a[1, 0, 0, 1] + a[2, 0, 1, 0])
            + sq(a[0, 0, 0, 1] + a[2, 1, 0, 0])
        )
        trace_1 = (
            sq(a[0, 1, 1, 0] + a[2, 0, 1, 1])
            + sq(a[0, 1, 0, 1] + a[1, 0, 1, 1])
            + sq(a[1, 1, 1, 0] + a[2, 1, 0, 1])
        )
        shear_1 = (
            sq(a[0, 0, 1, 1] + a[1, 1, 0, 1])
            + sq(a[1, 1, 0, 1] + a[2, 1, 1, 0])
            + sq(a[0, 0, 1, 1] + a[2, 1, 1, 0])
        )
        stiff = (
            ((lam / 16) * trace + (mu / 8) * axial)
            + ((mu / 16) * shear + (lam / 48) * trace_1)
            + ((mu / 16) * bend + (mu / 48) * shear_1)
            + ((lam + 4 * mu) / 144) * q3
        )
        return stiff, mass

    def element_pass(m, _):
        for pairs in range(2):
            groups = (2 * pairs, 2 * pairs + 1)

            def body(x, held):
                nexts = []
                for i, g in enumerate(groups):
                    later = sum((plane(3 * m + c, x + 1, g) for c in range(3)), ())
                    nexts += later
                    stiff, mass = energies(held[12 * i : 12 * i + 12], later)
                    stiffs[m, x, 8 * g : 8 * g + 8, :] = stiff
                    mass_terms[m, x, 8 * g : 8 * g + 8, :] = mass
                return tuple(nexts)

            first = []
            for g in groups:
                first += sum((plane(3 * m + c, 0, g) for c in range(3)), ())
            lax.fori_loop(0, TX, body, tuple(first))
        return 0

    lax.fori_loop(0, 2, element_pass, 0)

    top_t = math.tanh(4.0)
    merge_z(0)
    eigs = [eig[m] for m in range(2)]

    def project(xb, acc):
        acc = list(acc)
        for i in range(4):
            x = 4 * xb + i
            xpos = mx * TX + x
            x1 = inside(xpos - 1, cx * TX) + inside(xpos + 1, cx * TX)
            x2 = inside(xpos - 2, cx * TX) + inside(xpos + 2, cx * TX)
            for g in range(4):
                rows = slice(8 * g, 8 * g + 8)
                inverse = 1.0 / (wparts[0, g] + x1 * wparts[1, g] + x2 * wparts[2, g])
                t = jnp.tanh(8.0 * ((fz[x, rows, :] + from_z(0, xb, i, g)) * inverse - 0.5))
                rho = (top_t + t) * (0.5 / top_t)
                slope = (1.0 - t * t) * inverse * (4.0 / top_t)
                cubic = (3.0 * (1.0 - 0.001)) * (rho * rho)
                for m in range(2):
                    mass = mass_terms[m, x, rows, :]
                    acc[m] = acc[m] + rho * mass
                    gp[m, x + 2, 8 + 8 * g : 16 + 8 * g, :] = (
                        cubic * stiffs[m, x, rows, :] - eigs[m] * mass
                    ) * slope
        return tuple(acc)

    masses = lax.fori_loop(0, 4, project, (zero, zero))
    for m in range(2):
        a_in[0, m : m + 1, :] = jnp.sum(masses[m], axis=0, keepdims=True)

    for o in FLAT:
        (xs, xd, xn), (ys, yd, yn) = X_SPAN[o[0]], Y_SPAN[o[1]]
        send(
            o,
            gp.at[:, pl.ds(xs + 2, xn), pl.ds(ys + 8, yn)],
            gp.at[:, pl.ds(xd, xn), pl.ds(yd, yn)],
            9,
        )
    flats = all_of(gp.at[:, pl.ds(0, 13), pl.ds(0, 16)], 9)
    sent.append(flats)

    def spread_sum(ref, count, device, sem):
        def start(k, _):
            pltpu.make_async_remote_copy(
                src_ref=ref.at[0],
                dst_ref=ref.at[k],
                send_sem=send_sem.at[sem],
                recv_sem=recv_sem.at[sem],
                device_id=device(k),
                device_id_type=MESH,
            ).start()
            return 0

        lax.fori_loop(1, count, start, 0)
        copy = all_of(ref.at[pl.ds(1, count - 1)], sem)
        sent.append(copy)
        return copy

    a_copies = spread_sum(a_in, a_count, a_device, 10)

    flats.wait_recv()
    clear_halo(gp, (slice(None),))
    stores = []
    for m in range(2):

        def put_grad(x, g, value, m=m):
            outs[m, x, 8 * g : 8 * g + 8, :] = value

        sweep(lambda p, a, b, m=m: gp[m, p, a:b, :], put_grad, z_out.at[1 + m])
        send_z(1 + m)
        if m == 0:
            a_copies.wait_recv()
            b_in[0] = jnp.sum(a_in[...], axis=0)
            b_copies = spread_sum(b_in, b_count, b_device, 11)

    for m in range(2):
        merge_z(1 + m)

        def finish(xb, _, m=m):
            for i in range(4):
                for g in range(4):
                    rows = slice(8 * g, 8 * g + 8)
                    outs[m, 4 * xb + i, rows, :] = outs[m, 4 * xb + i, rows, :] + from_z(
                        1 + m, xb, i, g
                    )
            return 0

        lax.fori_loop(0, 4, finish, 0)
        store = pltpu.make_async_copy(outs.at[m], raw_ref.at[m], out_sem.at[m])
        store.start()
        stores.append(store)

    b_copies.wait_recv()
    total = jnp.sum(jnp.sum(b_in[...], axis=0), axis=1, keepdims=True)
    total_ref[...] = jnp.broadcast_to(total, (2, 128))

    for copies in sent:
        copies.wait_send()
    for store in stores:
        store.wait()


def per_device(sizes, design, modes, eigenvalues):
    cx, cy, cz = sizes
    a_count, b_count = (cx // 2) * cz, 2 * cy
    count = float(cx * TX * cy * TY * cz * TZ)
    dma = pltpu.SemaphoreType.DMA

    def vmem(*shape):
        return pltpu.VMEM(shape, F32)

    raw, total = pl.pallas_call(
        lambda *refs: kernel(sizes, *refs),
        out_shape=(
            jax.ShapeDtypeStruct((2, TX, TY, TZ), F32),
            jax.ShapeDtypeStruct((2, 128), F32),
        ),
        in_specs=[pl.BlockSpec(memory_space=pl.ANY)] * 3,
        out_specs=(
            pl.BlockSpec(memory_space=pl.ANY),
            pl.BlockSpec(memory_space=pltpu.VMEM),
        ),
        scratch_shapes=[
            vmem(TX + 4, TY + 16, TZ),
            vmem(6, TX + 1, TY + 8, TZ),
            vmem(6, TX + 1, TY + 8, TZ),
            vmem(3, 8, 128),
            vmem(4, 3, 8, 128),
            vmem(3, 4, 8, 128),
            vmem(TX, TY, TZ),
            vmem(2, TX, TY, TZ),
            vmem(2, TX, TY, TZ),
            vmem(2, TX + 4, TY + 16, TZ),
            vmem(2, TX, TY, TZ),
            vmem(3, 2, 8, 128),
            vmem(3, 2, 8, 128),
            vmem(3, 2, 8, 128),
            vmem(a_count, 2, 128),
            vmem(b_count, 2, 128),
            pltpu.SMEM((2,), F32),
            dma((8,)),
            dma((2,)),
            dma((12,)),
            dma((12,)),
        ],
        compiler_params=pltpu.CompilerParams(
            collective_id=0, has_side_effects=True, vmem_limit_bytes=62 * 1024 * 1024
        ),
    )(design, modes.reshape(6, TX, TY, TZ), eigenvalues)
    return raw * (count / total[:, 0])[:, None, None, None]


def solution(mesh):
    sizes = tuple(mesh.shape[a] for a in AXES)
    return jax.shard_map(
        lambda design, modes, eigenvalues: per_device(sizes, design, modes, eigenvalues),
        mesh=mesh,
        in_specs=(P("gx", "gy", "gz"), P(None, None, "gx", "gy", "gz"), P()),
        out_specs=P(None, "gx", "gy", "gz"),
        check_vma=False,
    )
```

```python
import itertools
import math

import jax
import jax.numpy as jnp
from jax import lax
from jax.experimental import pallas as pl
from jax.experimental.pallas import tpu as pltpu
from jax.sharding import PartitionSpec as P

AXES = ("gx", "gy", "gz")
MESH = pl.DeviceIdType.MESH
TX, TY, TZ = 16, 32, 128
FLAT = [o for o in itertools.product((-1, 0, 1), (-1, 0, 1), (0,)) if o != (0, 0, 0)]
BELOW = [(0, 0, -1), (0, -1, -1), (-1, 0, -1), (-1, -1, -1)]
F32 = jnp.float32


def weight(i, j, k):
    return max(0.0, 3.0 - math.sqrt(i * i + j * j + k * k))


X_SPAN = {-1: (0, TX + 2, 2), 0: (0, 2, TX), 1: (TX - 2, 0, 2)}
Y_SPAN = {-1: (0, TY + 8, 2), 0: (0, 8, TY), 1: (TY - 2, 6, 2)}


def combine(values, weights):
    total = None
    for value, w in zip(values, weights):
        if w == 0.0:
            continue
        total = w * value if total is None else total + w * value
    return total


def loop(n, body, init, by=1):
    def block(q, carry):
        for i in range(by):
            carry = body(q * by + i, carry)
        return carry

    return block(0, init) if by == n else lax.fori_loop(0, n // by, block, init)


def kernel(
    sizes,
    design_ref,
    modes_ref,
    eig_ref,
    raw_ref,
    total_ref,
    dp,
    mb,
    mz,
    face,
    from_hi,
    wparts,
    fz,
    stiffs,
    mass_terms,
    gp,
    outs,
    z_out,
    z_up,
    z_down,
    a_in,
    b_in,
    eig,
    local_sem,
    out_sem,
    send_sem,
    recv_sem,
):
    cx, cy, cz = sizes
    me = tuple(lax.axis_index(a) for a in AXES)
    mx, my, mzi = me

    def near(o):
        return tuple(m + d if d else m for m, d in zip(me, o))

    def there(o):
        ok = None
        for m, d, size in zip(me, o, sizes):
            if d:
                here = m > 0 if d < 0 else m < size - 1
                ok = here if ok is None else ok & here
        return ok

    def opposite(o):
        return tuple(-d for d in o)

    a_count, b_count = (cx // 2) * cz, 2 * cy
    a_slot = (mx // 2) * cz + mzi
    b_slot = lax.rem(mx, 2) * cy + my

    def a_device(slot):
        return ((slot // cz) * 2 + lax.rem(mx, 2), my, lax.rem(slot, cz))

    def b_device(slot):
        return ((mx // 2) * 2 + slot // cy, lax.rem(slot, cy), mzi)

    barrier = pltpu.get_barrier_semaphore()

    def greet(device):
        pl.semaphore_signal(barrier, inc=1, device_id=device, device_id_type=MESH)

    heard = a_count - 1 + b_count - 1
    for o in FLAT + [(0, 0, 1), (0, 0, -1)] + BELOW[1:]:
        heard = heard + there(o).astype(jnp.int32)
    for o in FLAT + [(0, 0, 1), (0, 0, -1)] + [opposite(o) for o in BELOW[1:]]:

        @pl.when(there(o))
        def _(o=o):
            greet(near(o))

    loads = [
        pltpu.make_async_copy(design_ref, dp.at[pl.ds(2, TX), pl.ds(8, TY)], local_sem.at[0])
    ]
    for c in range(6):
        loads.append(
            pltpu.make_async_copy(
                modes_ref.at[c], mb.at[c, pl.ds(0, TX), pl.ds(0, TY)], local_sem.at[1 + c]
            )
        )
    loads.append(pltpu.make_async_copy(eig_ref, eig, local_sem.at[7]))
    for load in loads:
        load.start()

    def greet_a(k, _):
        greet(a_device(lax.rem(a_slot + k, a_count)))
        return 0

    def greet_b(k, _):
        greet(b_device(lax.rem(b_slot + k, b_count)))
        return 0

    lax.fori_loop(1, a_count, greet_a, 0)
    lax.fori_loop(1, b_count, greet_b, 0)

    lane = lax.broadcasted_iota(jnp.int32, (8, 128), 1)
    quad = lax.shift_right_logical(lax.rem(lane + 2, 128), 2)
    first_two, last_two = lane < 2, lane >= 126
    zero = jnp.zeros((8, 128), F32)

    for load in loads:
        load.wait()

    def pack_modes(x, carry):
        carry = list(carry)
        for c in range(6):
            for g in range(4):
                k = (c % 2) * 64 + 4 * x + g
                r = pltpu.roll(mb[c, x, 8 * g : 8 * g + 8, :], k, 1)
                carry[c // 2] = jnp.where(lane == k, r, carry[c // 2])
        return tuple(carry)

    packed = loop(TX, pack_modes, (zero, zero, zero), TX)
    for i in range(3):
        face[i] = packed[i]

    pl.semaphore_wait(barrier, heard)

    sent = []

    def remote(src, dst, sem, device):
        return pltpu.make_async_remote_copy(
            src_ref=src,
            dst_ref=dst,
            send_sem=send_sem.at[sem],
            recv_sem=recv_sem.at[sem],
            device_id=device,
            device_id_type=MESH,
        )

    def send(o, src, dst, sem):
        @pl.when(there(o))
        def _():
            remote(src, dst, sem, near(o)).start()

        def sent_all():
            @pl.when(there(o))
            def _():
                remote(src, dst, sem, near(o)).wait_send()

        def received():
            @pl.when(there(opposite(o)))
            def _():
                remote(src, dst, sem, near(o)).wait_recv()

        sent.append(sent_all)
        return received

    def send_flats(src, dst, lead, shift, sem):
        waits = []
        for i, o in enumerate(FLAT):
            (xs, xd, xn), (ys, yd, yn) = X_SPAN[o[0]], Y_SPAN[o[1]]
            waits.append(
                send(
                    o,
                    src.at[lead + (pl.ds(xs + shift[0], xn), pl.ds(ys + shift[1], yn))],
                    dst.at[lead + (pl.ds(xd, xn), pl.ds(yd, yn))],
                    sem + i,
                )
            )
        return waits

    design_waits = send_flats(design_ref, dp, (), (0, 0), 0)
    mode_waits = []
    for i, o in enumerate(((-1, 0, 0), (0, -1, 0), (-1, -1, 0))):
        dx, dy, _ = o
        xs = pl.ds(0, 1) if dx else pl.ds(0, TX)
        xd = pl.ds(TX, 1) if dx else pl.ds(0, TX)
        ys = pl.ds(0, 1) if dy else pl.ds(0, TY)
        yd = pl.ds(TY, 1) if dy else pl.ds(0, TY)
        mode_waits.append(send(o, modes_ref.at[:, xs, ys], mb.at[:, xd, yd], 8 + i))
    for i, o in enumerate(BELOW):
        mode_waits.append(send(o, face, from_hi.at[-2 * o[0] - o[1]], 11 + i))

    def shift_modes(x, _):
        for c in range(6):
            for g in range(4):
                rows = slice(8 * g, 8 * g + 8)
                mz[c, x, rows, :] = pltpu.roll(mb[c, x, rows, :], 127, 1)
        return 0

    loop(TX, shift_modes, 0, 4)

    def inside(cell, total):
        return ((cell >= 0) & (cell < total)).astype(F32)

    zpos = mzi * TZ + lane
    z1 = inside(zpos - 1, cz * TZ) + inside(zpos + 1, cz * TZ)
    z2 = inside(zpos - 2, cz * TZ) + inside(zpos + 2, cz * TZ)
    for g in range(4):
        ypos = my * TY + 8 * g + lax.broadcasted_iota(jnp.int32, (8, 128), 0)
        y1 = inside(ypos - 1, cy * TY) + inside(ypos + 1, cy * TY)
        y2 = inside(ypos - 2, cy * TY) + inside(ypos + 2, cy * TY)
        for i in range(3):
            rows = [
                weight(i, j, 0) + weight(i, j, 1) * z1 + weight(i, j, 2) * z2 for j in range(3)
            ]
            wparts[i, g] = rows[0] + y1 * rows[1] + y2 * rows[2]

    def clear(ref, index, cond):
        @pl.when(cond)
        def _():
            ref[index] = jnp.zeros_like(ref[index])

    def clear_halo(ref, lead):
        clear(ref, lead + (slice(0, 2),), mx == 0)
        clear(ref, lead + (slice(TX + 2, TX + 4),), mx == cx - 1)
        clear(ref, lead + (slice(None), slice(0, 8)), my == 0)
        clear(ref, lead + (slice(None), slice(TY + 8, TY + 16)), my == cy - 1)

    order = ((0, 0), (0, 1), (1, 1), (0, 2), (1, 2), (2, 2))

    def sweep(load, put, packs):
        packs[0] = zero
        packs[1] = zero

        def body(xb, _):
            held = packs[xb // 2]
            for g in range(4):
                top = 8 + 8 * g
                a = {}
                for t in range(8):
                    p = 4 * xb + t
                    a[t, 0] = load(p, top, top + 8)
                    a[t, 1] = load(p, top - 1, top + 7) + load(p, top + 1, top + 9)
                    a[t, 2] = load(p, top - 2, top + 6) + load(p, top + 2, top + 10)
                for i in range(4):
                    b = {}
                    for j in range(3):
                        b[0, j] = a[i + 2, j]
                        b[1, j] = a[i + 1, j] + a[i + 3, j]
                        b[2, j] = a[i, j] + a[i + 4, j]
                    grouped = [b[u, v] if u == v else b[u, v] + b[v, u] for u, v in order]
                    e0, e1, e2 = (
                        combine(grouped, [weight(u, v, k) for u, v in order]) for k in range(3)
                    )
                    up, down = pltpu.roll(e1, 1, 1), pltpu.roll(e1, 127, 1)
                    up2, down2 = pltpu.roll(e2, 2, 1), pltpu.roll(e2, 126, 1)
                    out = jnp.where(lane < 1, up, jnp.where(lane >= 127, down, 0.0)) + jnp.where(
                        first_two, up2, jnp.where(last_two, down2, 0.0)
                    )
                    put(4 * xb + i, g, (e0 + ((up + down) + (up2 + down2))) - out)
                    k = lax.rem(xb, 2) * 16 + 4 * i + g
                    held = jnp.where(quad == k, pltpu.roll(out, 4 * k, 1), held)
            packs[xb // 2] = held
            return 0

        lax.fori_loop(0, 4, body, 0)

    def send_z(f):
        return (
            send((0, 0, -1), z_out.at[f], z_up.at[f], 23 + f),
            send((0, 0, 1), z_out.at[f], z_down.at[f], 26 + f),
        )

    def merge_z(f, waits):
        for wait in waits:
            wait()
        clear(z_up, f, mzi == cz - 1)
        clear(z_down, f, mzi == 0)
        for h in range(2):
            z_up[f, h] = jnp.where(lax.rem(lane, 4) >= 2, z_up[f, h], z_down[f, h])

    def from_z(f, xb, i, g):
        k = lax.rem(xb, 2) * 16 + 4 * i + g
        r = pltpu.roll(z_up[f, xb // 2], lax.rem(128 - 4 * k, 128), 1)
        return jnp.where(first_two | last_two, r, 0.0)

    for wait in design_waits:
        wait()
    clear_halo(dp, ())

    def put_design(x, g, value):
        fz[x, 8 * g : 8 * g + 8, :] = value

    sweep(lambda p, a, b: dp[p, a:b, :], put_design, z_out.at[0])
    z_waits = [send_z(0)]

    for wait in mode_waits:
        wait()
    for o in BELOW:
        clear(from_hi, -2 * o[0] - o[1], jnp.logical_not(there(opposite(o))))
    clear(mb, (slice(None), TX), mx == cx - 1)
    clear(mb, (slice(None), slice(None), slice(TY, TY + 8)), my == cy - 1)
    last = lane >= 127

    def patch_modes(x, _):
        for c in range(6):
            for g in range(5):
                k = (c % 2) * 64 + 4 * x + g % 4
                rows = slice(8 * g, 8 * g + 8)
                h = pltpu.roll(from_hi[g // 4, c // 2], lax.rem(255 - k, 128), 1)
                own = pltpu.roll(mb[c, x, rows, :], 127, 1) if g == 4 else mz[c, x, rows, :]
                mz[c, x, rows, :] = jnp.where(last, h, own)
        return 0

    loop(TX, patch_modes, 0, 2)

    def patch_end(c, _):
        for g in range(5):
            k = lax.rem(c, 2) * 64 + g % 4
            rows = slice(8 * g, 8 * g + 8)
            h = pltpu.roll(from_hi[2 + g // 4, c // 2], lax.rem(255 - k, 128), 1)
            mz[c, TX, rows, :] = jnp.where(last, h, pltpu.roll(mb[c, TX, rows, :], 127, 1))
        return 0

    loop(6, patch_end, 0, 3)

    factor = 1.0 / (1.3 * 0.4)
    lam, mu = 0.3 * factor, 0.2 * factor

    def plane(c, x, g):
        a, b = 8 * g, 8 * g + 8
        v0, v1 = mb[c, x, a:b, :], mb[c, x, a + 1 : b + 1, :]
        w0, w1 = mz[c, x, a:b, :], mz[c, x, a + 1 : b + 1, :]
        vs, vd, ws, wd = v0 + v1, v1 - v0, w0 + w1, w1 - w0
        return vs + ws, ws - vs, vd + wd, wd - vd

    def energies(now, later):
        a = {}
        for c in range(3):
            for q, (j, k) in enumerate(((0, 0), (0, 1), (1, 0), (1, 1))):
                a[c, 0, j, k] = now[4 * c + q] + later[4 * c + q]
                a[c, 1, j, k] = later[4 * c + q] - now[4 * c + q]
        s = {key: v * v for key, v in a.items()}

        def sq(v):
            return v * v

        q0 = s[0, 0, 0, 0] + s[1, 0, 0, 0] + s[2, 0, 0, 0]
        axial = s[0, 1, 0, 0] + s[1, 0, 1, 0] + s[2, 0, 0, 1]
        q1 = axial + (
            (s[0, 0, 1, 0] + s[0, 0, 0, 1])
            + (s[1, 1, 0, 0] + s[1, 0, 0, 1])
            + (s[2, 1, 0, 0] + s[2, 0, 1, 0])
        )
        bend = (
            (s[0, 1, 1, 0] + s[0, 1, 0, 1])
            + (s[1, 1, 1, 0] + s[1, 0, 1, 1])
            + (s[2, 1, 0, 1] + s[2, 0, 1, 1])
        )
        q2 = bend + (s[0, 0, 1, 1] + s[1, 1, 0, 1] + s[2, 1, 1, 0])
        q3 = s[0, 1, 1, 1] + s[1, 1, 1, 1] + s[2, 1, 1, 1]
        mass = (1 / 64) * q0 + (1 / 192) * q1 + ((1 / 576) * q2 + (1 / 1728) * q3)
        trace = sq(a[0, 1, 0, 0] + a[1, 0, 1, 0] + a[2, 0, 0, 1])
        shear = (
            sq(a[0, 0, 1, 0] + a[1, 1, 0, 0])
            + sq(a[1, 0, 0, 1] + a[2, 0, 1, 0])
            + sq(a[0, 0, 0, 1] + a[2, 1, 0, 0])
        )
        trace_1 = (
            sq(a[0, 1, 1, 0] + a[2, 0, 1, 1])
            + sq(a[0, 1, 0, 1] + a[1, 0, 1, 1])
            + sq(a[1, 1, 1, 0] + a[2, 1, 0, 1])
        )
        shear_1 = (
            sq(a[0, 0, 1, 1] + a[1, 1, 0, 1])
            + sq(a[1, 1, 0, 1] + a[2, 1, 1, 0])
            + sq(a[0, 0, 1, 1] + a[2, 1, 1, 0])
        )
        stiff = (
            ((lam / 16) * trace + (mu / 8) * axial)
            + ((mu / 16) * shear + (lam / 48) * trace_1)
            + ((mu / 16) * bend + (mu / 48) * shear_1)
            + ((lam + 4 * mu) / 144) * q3
        )
        return stiff, mass

    def element_pass(m, _):
        for pairs in range(2):
            groups = (2 * pairs, 2 * pairs + 1)

            def body(x, held):
                nexts = []
                for i, g in enumerate(groups):
                    later = sum((plane(3 * m + c, x + 1, g) for c in range(3)), ())
                    nexts += later
                    stiff, mass = energies(held[12 * i : 12 * i + 12], later)
                    stiffs[m, x, 8 * g : 8 * g + 8, :] = stiff
                    mass_terms[m, x, 8 * g : 8 * g + 8, :] = mass
                return tuple(nexts)

            first = []
            for g in groups:
                first += sum((plane(3 * m + c, 0, g) for c in range(3)), ())
            lax.fori_loop(0, TX, body, tuple(first))
        return 0

    lax.fori_loop(0, 2, element_pass, 0)

    top_t = math.tanh(4.0)
    merge_z(0, z_waits[0])
    eigs = [eig[m] for m in range(2)]

    def project(xb, acc):
        acc = list(acc)
        for i in range(4):
            x = 4 * xb + i
            xpos = mx * TX + x
            x1 = inside(xpos - 1, cx * TX) + inside(xpos + 1, cx * TX)
            x2 = inside(xpos - 2, cx * TX) + inside(xpos + 2, cx * TX)
            for g in range(4):
                rows = slice(8 * g, 8 * g + 8)
                inverse = 1.0 / (wparts[0, g] + x1 * wparts[1, g] + x2 * wparts[2, g])
                t = jnp.tanh(8.0 * ((fz[x, rows, :] + from_z(0, xb, i, g)) * inverse - 0.5))
                rho = (top_t + t) * (0.5 / top_t)
                slope = (1.0 - t * t) * inverse * (4.0 / top_t)
                cubic = (3.0 * (1.0 - 0.001)) * (rho * rho)
                for m in range(2):
                    mass = mass_terms[m, x, rows, :]
                    acc[m] = acc[m] + rho * mass
                    gp[m, x + 2, 8 + 8 * g : 16 + 8 * g, :] = (
                        cubic * stiffs[m, x, rows, :] - eigs[m] * mass
                    ) * slope
        return tuple(acc)

    masses = lax.fori_loop(0, 4, project, (zero, zero))
    for m in range(2):
        a_in[a_slot, m : m + 1, :] = jnp.sum(masses[m], axis=0, keepdims=True)

    def spread_sum(ref, count, slot, device, sem):
        def start(k, _):
            @pl.when(k != slot)
            def _():
                remote(ref.at[slot], ref.at[slot], sem, device(k)).start()

            return 0

        lax.fori_loop(0, count, start, 0)
        return remote(ref.at[pl.ds(0, count - 1)], ref.at[pl.ds(0, count - 1)], sem, me)

    a_copies = spread_sum(a_in, a_count, a_slot, a_device, 29)
    flats = send_flats(gp, gp, (slice(None),), (2, 8), 15)

    for wait in flats:
        wait()
    clear_halo(gp, (slice(None),))
    stores = []
    for m in range(2):

        def put_grad(x, g, value, m=m):
            outs[m, x, 8 * g : 8 * g + 8, :] = value

        sweep(lambda p, a, b, m=m: gp[m, p, a:b, :], put_grad, z_out.at[1 + m])
        z_waits.append(send_z(1 + m))

    a_copies.wait_recv()
    b_in[b_slot] = jnp.sum(a_in[...], axis=0)
    b_copies = spread_sum(b_in, b_count, b_slot, b_device, 30)

    for m in range(2):
        merge_z(1 + m, z_waits[1 + m])

        def finish(xb, _, m=m):
            for i in range(4):
                for g in range(4):
                    rows = slice(8 * g, 8 * g + 8)
                    outs[m, 4 * xb + i, rows, :] = outs[m, 4 * xb + i, rows, :] + from_z(
                        1 + m, xb, i, g
                    )
            return 0

        lax.fori_loop(0, 4, finish, 0)
        store = pltpu.make_async_copy(outs.at[m], raw_ref.at[m], out_sem.at[m])
        store.start()
        stores.append(store)

    b_copies.wait_recv()
    total = jnp.sum(jnp.sum(b_in[...], axis=0), axis=1, keepdims=True)
    total_ref[...] = jnp.broadcast_to(total, (2, 128))

    for wait in sent:
        wait()
    a_copies.wait_send()
    b_copies.wait_send()
    for store in stores:
        store.wait()


def per_device(sizes, design, modes, eigenvalues):
    cx, cy, cz = sizes
    a_count, b_count = (cx // 2) * cz, 2 * cy
    count = float(cx * TX * cy * TY * cz * TZ)
    dma = pltpu.SemaphoreType.DMA

    def vmem(*shape):
        return pltpu.VMEM(shape, F32)

    raw, total = pl.pallas_call(
        lambda *refs: kernel(sizes, *refs),
        out_shape=(
            jax.ShapeDtypeStruct((2, TX, TY, TZ), F32),
            jax.ShapeDtypeStruct((2, 128), F32),
        ),
        in_specs=[pl.BlockSpec(memory_space=pl.ANY)] * 3,
        out_specs=(
            pl.BlockSpec(memory_space=pl.ANY),
            pl.BlockSpec(memory_space=pltpu.VMEM),
        ),
        scratch_shapes=[
            vmem(TX + 4, TY + 16, TZ),
            vmem(6, TX + 1, TY + 8, TZ),
            vmem(6, TX + 1, TY + 8, TZ),
            vmem(3, 8, 128),
            vmem(4, 3, 8, 128),
            vmem(3, 4, 8, 128),
            vmem(TX, TY, TZ),
            vmem(2, TX, TY, TZ),
            vmem(2, TX, TY, TZ),
            vmem(2, TX + 4, TY + 16, TZ),
            vmem(2, TX, TY, TZ),
            vmem(3, 2, 8, 128),
            vmem(3, 2, 8, 128),
            vmem(3, 2, 8, 128),
            vmem(a_count, 2, 128),
            vmem(b_count, 2, 128),
            pltpu.SMEM((2,), F32),
            dma((8,)),
            dma((2,)),
            dma((31,)),
            dma((31,)),
        ],
        compiler_params=pltpu.CompilerParams(
            collective_id=0, has_side_effects=True, vmem_limit_bytes=62 * 1024 * 1024
        ),
    )(design, modes.reshape(6, TX, TY, TZ), eigenvalues)
    return raw * (count / total[:, 0])[:, None, None, None]


def solution(mesh):
    sizes = tuple(mesh.shape[a] for a in AXES)
    return jax.shard_map(
        lambda design, modes, eigenvalues: per_device(sizes, design, modes, eigenvalues),
        mesh=mesh,
        in_specs=(P("gx", "gy", "gz"), P(None, None, "gx", "gy", "gz"), P()),
        out_specs=P(None, "gx", "gy", "gz"),
        check_vma=False,
    )
```

```python
import itertools
import math

import jax
import jax.numpy as jnp
from jax import lax
from jax.experimental import pallas as pl
from jax.experimental.pallas import tpu as pltpu
from jax.sharding import PartitionSpec as P

AXES = ("gx", "gy", "gz")
MESH = pl.DeviceIdType.MESH
TX, TY, TZ = 16, 32, 128
FLAT = [o for o in itertools.product((-1, 0, 1), (-1, 0, 1), (0,)) if o != (0, 0, 0)]
SIDES = [(-1, 0, 0), (0, -1, 0), (-1, -1, 0)]
BELOW = [(0, 0, -1), (0, -1, -1), (-1, 0, -1), (-1, -1, -1)]
F32 = jnp.float32


def weight(i, j, k):
    return max(0.0, 3.0 - math.sqrt(i * i + j * j + k * k))


X_SPAN = {-1: (0, TX + 2, 2), 0: (0, 2, TX), 1: (TX - 2, 0, 2)}
Y_SPAN = {-1: (0, TY + 8, 2), 0: (0, 8, TY), 1: (TY - 2, 6, 2)}


def combine(values, weights):
    total = None
    for value, w in zip(values, weights):
        if w == 0.0:
            continue
        total = w * value if total is None else total + w * value
    return total


def loop(n, body, init, by=1):
    def block(q, carry):
        for i in range(by):
            carry = body(q * by + i, carry)
        return carry

    return block(0, init) if by == n else lax.fori_loop(0, n // by, block, init)


def kernel(
    sizes,
    design_ref,
    modes_ref,
    eig_ref,
    raw_ref,
    scale_ref,
    dp,
    mb,
    mz,
    face,
    from_hi,
    from_side,
    edge,
    wparts,
    fz,
    stiffs,
    mass_terms,
    gp,
    outs,
    z_out,
    z_up,
    z_down,
    a_in,
    b_in,
    eig,
    local_sem,
    out_sem,
    send_sem,
    recv_sem,
):
    cx, cy, cz = sizes
    count = float(cx * TX * cy * TY * cz * TZ)
    me = tuple(lax.axis_index(a) for a in AXES)
    mx, my, mzi = me

    def near(o):
        return tuple(m + d if d else m for m, d in zip(me, o))

    def there(o):
        ok = None
        for m, d, size in zip(me, o, sizes):
            if d:
                here = m > 0 if d < 0 else m < size - 1
                ok = here if ok is None else ok & here
        return ok

    def opposite(o):
        return tuple(-d for d in o)

    a_count, b_count = (cx // 2) * cz, 2 * cy
    a_slot = (mx // 2) * cz + mzi
    b_slot = lax.rem(mx, 2) * cy + my

    def a_device(slot):
        return ((slot // cz) * 2 + lax.rem(mx, 2), my, lax.rem(slot, cz))

    def b_device(slot):
        return ((mx // 2) * 2 + slot // cy, lax.rem(slot, cy), mzi)

    barrier = pltpu.get_barrier_semaphore()

    def greet(device):
        pl.semaphore_signal(barrier, inc=1, device_id=device, device_id_type=MESH)

    heard = a_count - 1 + b_count - 1
    for o in FLAT + [(0, 0, 1), (0, 0, -1)] + BELOW[1:]:
        heard = heard + there(o).astype(jnp.int32)
    for o in FLAT + [(0, 0, 1), (0, 0, -1)] + [opposite(o) for o in BELOW[1:]]:

        @pl.when(there(o))
        def _(o=o):
            greet(near(o))

    loads = [
        pltpu.make_async_copy(design_ref, dp.at[pl.ds(2, TX), pl.ds(8, TY)], local_sem.at[0])
    ]
    for c in range(6):
        loads.append(
            pltpu.make_async_copy(
                modes_ref.at[c], mb.at[c, pl.ds(0, TX), pl.ds(0, TY)], local_sem.at[1 + c]
            )
        )
    loads.append(pltpu.make_async_copy(eig_ref, eig, local_sem.at[7]))
    for load in loads:
        load.start()

    def greet_a(k, _):
        greet(a_device(lax.rem(a_slot + k, a_count)))
        return 0

    def greet_b(k, _):
        greet(b_device(lax.rem(b_slot + k, b_count)))
        return 0

    lax.fori_loop(1, a_count, greet_a, 0)
    lax.fori_loop(1, b_count, greet_b, 0)

    lane = lax.broadcasted_iota(jnp.int32, (8, 128), 1)
    quad = lax.shift_right_logical(lax.rem(lane + 2, 128), 2)
    first_two, last_two = lane < 2, lane >= 126
    zero = jnp.zeros((8, 128), F32)

    pl.semaphore_wait(barrier, heard)

    sent = []

    def remote(src, dst, sem, device):
        return pltpu.make_async_remote_copy(
            src_ref=src,
            dst_ref=dst,
            send_sem=send_sem.at[sem],
            recv_sem=recv_sem.at[sem],
            device_id=device,
            device_id_type=MESH,
        )

    def send(o, src, dst, sem):
        @pl.when(there(o))
        def _():
            remote(src, dst, sem, near(o)).start()

        def sent_all():
            @pl.when(there(o))
            def _():
                remote(src, dst, sem, near(o)).wait_send()

        def received():
            @pl.when(there(opposite(o)))
            def _():
                remote(src, dst, sem, near(o)).wait_recv()

        sent.append(sent_all)
        return received

    def send_flats(src, dst, lead, shift, sem):
        waits = []
        for i, o in enumerate(FLAT):
            (xs, xd, xn), (ys, yd, yn) = X_SPAN[o[0]], Y_SPAN[o[1]]
            waits.append(
                send(
                    o,
                    src.at[lead + (pl.ds(xs + shift[0], xn), pl.ds(ys + shift[1], yn))],
                    dst.at[lead + (pl.ds(xd, xn), pl.ds(yd, yn))],
                    sem + i,
                )
            )
        return waits

    design_waits = send_flats(design_ref, dp, (), (0, 0), 0)
    mode_waits = []
    for i, o in enumerate(SIDES):
        dx, dy, _ = o
        xs = pl.ds(0, 1) if dx else pl.ds(0, TX)
        xd = pl.ds(TX, 1) if dx else pl.ds(0, TX)
        ys = pl.ds(0, 1) if dy else pl.ds(0, TY)
        yd = pl.ds(TY, 1) if dy else pl.ds(0, TY)
        mode_waits.append(send(o, modes_ref.at[:, xs, ys], mb.at[:, xd, yd], 8 + i))

    for load in loads:
        load.wait()

    def pack_modes(x, carry):
        first, final = (list(v) for v in carry)
        for c in range(6):
            for g in range(4):
                k = (c // 3) * 64 + 4 * x + g
                r = pltpu.roll(mb[c, x, 8 * g : 8 * g + 8, :], k, 1)
                first[c % 3] = jnp.where(lane == k, r, first[c % 3])
                final[c % 3] = jnp.where(lane == (k + 127) % 128, r, final[c % 3])
        return tuple(first), tuple(final)

    first, final = loop(TX, pack_modes, ((zero,) * 3, (zero,) * 3), TX)
    for c in range(3):
        face[0, c] = first[c]
        face[1, c] = pltpu.roll(final[c], 1, 1)

    face_waits = []
    for i, o in enumerate(BELOW):
        face_waits.append(send(o, face.at[0], from_hi.at[-2 * o[0] - o[1]], 11 + i))
    for i, o in enumerate(SIDES):
        face_waits.append(send(o, face.at[1], from_side.at[-2 * o[0] - o[1]], 31 + i))

    def shift_modes(x, _):
        for c in range(6):
            for g in range(4):
                rows = slice(8 * g, 8 * g + 8)
                mz[c, x, rows, :] = pltpu.roll(mb[c, x, rows, :], 127, 1)
        return 0

    loop(TX, shift_modes, 0, 4)

    def inside(cell, total):
        return ((cell >= 0) & (cell < total)).astype(F32)

    zpos = mzi * TZ + lane
    z1 = inside(zpos - 1, cz * TZ) + inside(zpos + 1, cz * TZ)
    z2 = inside(zpos - 2, cz * TZ) + inside(zpos + 2, cz * TZ)
    for g in range(4):
        ypos = my * TY + 8 * g + lax.broadcasted_iota(jnp.int32, (8, 128), 0)
        y1 = inside(ypos - 1, cy * TY) + inside(ypos + 1, cy * TY)
        y2 = inside(ypos - 2, cy * TY) + inside(ypos + 2, cy * TY)
        for i in range(3):
            rows = [
                weight(i, j, 0) + weight(i, j, 1) * z1 + weight(i, j, 2) * z2 for j in range(3)
            ]
            wparts[i, g] = rows[0] + y1 * rows[1] + y2 * rows[2]

    def clear(ref, index, cond):
        @pl.when(cond)
        def _():
            ref[index] = jnp.zeros_like(ref[index])

    def clear_halo(ref, lead):
        clear(ref, lead + (slice(0, 2),), mx == 0)
        clear(ref, lead + (slice(TX + 2, TX + 4),), mx == cx - 1)
        clear(ref, lead + (slice(None), slice(0, 8)), my == 0)
        clear(ref, lead + (slice(None), slice(TY + 8, TY + 16)), my == cy - 1)

    order = ((0, 0), (0, 1), (1, 1), (0, 2), (1, 2), (2, 2))

    def sweep(load, put, packs):
        packs[0] = zero
        packs[1] = zero

        def body(xb, _):
            held = packs[xb // 2]
            for g in range(4):
                top = 8 + 8 * g
                a = {}
                for t in range(8):
                    p = 4 * xb + t
                    a[t, 0] = load(p, top, top + 8)
                    a[t, 1] = load(p, top - 1, top + 7) + load(p, top + 1, top + 9)
                    a[t, 2] = load(p, top - 2, top + 6) + load(p, top + 2, top + 10)
                for i in range(4):
                    b = {}
                    for j in range(3):
                        b[0, j] = a[i + 2, j]
                        b[1, j] = a[i + 1, j] + a[i + 3, j]
                        b[2, j] = a[i, j] + a[i + 4, j]
                    grouped = [b[u, v] if u == v else b[u, v] + b[v, u] for u, v in order]
                    e0, e1, e2 = (
                        combine(grouped, [weight(u, v, k) for u, v in order]) for k in range(3)
                    )
                    up, down = pltpu.roll(e1, 1, 1), pltpu.roll(e1, 127, 1)
                    up2, down2 = pltpu.roll(e2, 2, 1), pltpu.roll(e2, 126, 1)
                    out = jnp.where(lane < 1, up, jnp.where(lane >= 127, down, 0.0)) + jnp.where(
                        first_two, up2, jnp.where(last_two, down2, 0.0)
                    )
                    put(4 * xb + i, g, (e0 + ((up + down) + (up2 + down2))) - out)
                    k = lax.rem(xb, 2) * 16 + 4 * i + g
                    held = jnp.where(quad == k, pltpu.roll(out, 4 * k, 1), held)
            packs[xb // 2] = held
            return 0

        lax.fori_loop(0, 4, body, 0)

    def send_z(f):
        return (
            send((0, 0, -1), z_out.at[f], z_up.at[f], 23 + f),
            send((0, 0, 1), z_out.at[f], z_down.at[f], 26 + f),
        )

    def merge_z(f, waits):
        for wait in waits:
            wait()
        clear(z_up, f, mzi == cz - 1)
        clear(z_down, f, mzi == 0)
        for h in range(2):
            z_up[f, h] = jnp.where(lax.rem(lane, 4) >= 2, z_up[f, h], z_down[f, h])

    def from_z(f, xb, i, g):
        k = lax.rem(xb, 2) * 16 + 4 * i + g
        r = pltpu.roll(z_up[f, xb // 2], lax.rem(128 - 4 * k, 128), 1)
        return jnp.where(first_two | last_two, r, 0.0)

    for wait in design_waits:
        wait()
    clear_halo(dp, ())

    def put_design(x, g, value):
        fz[x, 8 * g : 8 * g + 8, :] = value

    sweep(lambda p, a, b: dp[p, a:b, :], put_design, z_out.at[0])
    z_waits = [send_z(0)]

    for wait in mode_waits:
        wait()
    clear(mb, (slice(None), TX), mx == cx - 1)
    clear(mb, (slice(None), slice(None), slice(TY, TY + 8)), my == cy - 1)

    def shift_halo(c, _):
        for x in range(TX + 1):
            mz[c, x, TY : TY + 8, :] = pltpu.roll(mb[c, x, TY : TY + 8, :], 127, 1)
        for g in range(4):
            rows = slice(8 * g, 8 * g + 8)
            mz[c, TX, rows, :] = pltpu.roll(mb[c, TX, rows, :], 127, 1)
        return 0

    loop(6, shift_halo, 0, 2)

    factor = 1.0 / (1.3 * 0.4)
    lam, mu = 0.3 * factor, 0.2 * factor

    def across(v0, v1, w0, w1):
        vs, vd, ws, wd = v0 + v1, v1 - v0, w0 + w1, w1 - w0
        return vs + ws, ws - vs, vd + wd, wd - vd

    def plane(c, x, g):
        a, b = 8 * g, 8 * g + 8
        v0, v1 = mb[c, x, a:b, :], mb[c, x, a + 1 : b + 1, :]
        return across(v0, v1, mz[c, x, a:b, :], mz[c, x, a + 1 : b + 1, :])

    def energies(now, later):
        a = {}
        for c in range(3):
            for q, (j, k) in enumerate(((0, 0), (0, 1), (1, 0), (1, 1))):
                a[c, 0, j, k] = now[4 * c + q] + later[4 * c + q]
                a[c, 1, j, k] = later[4 * c + q] - now[4 * c + q]
        s = {key: v * v for key, v in a.items()}

        def sq(v):
            return v * v

        q0 = s[0, 0, 0, 0] + s[1, 0, 0, 0] + s[2, 0, 0, 0]
        axial = s[0, 1, 0, 0] + s[1, 0, 1, 0] + s[2, 0, 0, 1]
        q1 = axial + (
            (s[0, 0, 1, 0] + s[0, 0, 0, 1])
            + (s[1, 1, 0, 0] + s[1, 0, 0, 1])
            + (s[2, 1, 0, 0] + s[2, 0, 1, 0])
        )
        bend = (
            (s[0, 1, 1, 0] + s[0, 1, 0, 1])
            + (s[1, 1, 1, 0] + s[1, 0, 1, 1])
            + (s[2, 1, 0, 1] + s[2, 0, 1, 1])
        )
        q2 = bend + (s[0, 0, 1, 1] + s[1, 1, 0, 1] + s[2, 1, 1, 0])
        q3 = s[0, 1, 1, 1] + s[1, 1, 1, 1] + s[2, 1, 1, 1]
        mass = (1 / 64) * q0 + (1 / 192) * q1 + ((1 / 576) * q2 + (1 / 1728) * q3)
        trace = sq(a[0, 1, 0, 0] + a[1, 0, 1, 0] + a[2, 0, 0, 1])
        shear = (
            sq(a[0, 0, 1, 0] + a[1, 1, 0, 0])
            + sq(a[1, 0, 0, 1] + a[2, 0, 1, 0])
            + sq(a[0, 0, 0, 1] + a[2, 1, 0, 0])
        )
        trace_1 = (
            sq(a[0, 1, 1, 0] + a[2, 0, 1, 1])
            + sq(a[0, 1, 0, 1] + a[1, 0, 1, 1])
            + sq(a[1, 1, 1, 0] + a[2, 1, 0, 1])
        )
        shear_1 = (
            sq(a[0, 0, 1, 1] + a[1, 1, 0, 1])
            + sq(a[1, 1, 0, 1] + a[2, 1, 1, 0])
            + sq(a[0, 0, 1, 1] + a[2, 1, 1, 0])
        )
        stiff = (
            ((lam / 16) * trace + (mu / 8) * axial)
            + ((mu / 16) * shear + (lam / 48) * trace_1)
            + ((mu / 16) * bend + (mu / 48) * shear_1)
            + ((lam + 4 * mu) / 144) * q3
        )
        return stiff, mass

    def element_pass(m, _):
        for pairs in range(2):
            groups = (2 * pairs, 2 * pairs + 1)

            def body(x, held):
                nexts = []
                for i, g in enumerate(groups):
                    later = sum((plane(3 * m + c, x + 1, g) for c in range(3)), ())
                    nexts += later
                    stiff, mass = energies(held[12 * i : 12 * i + 12], later)
                    stiffs[m, x, 8 * g : 8 * g + 8, :] = stiff
                    mass_terms[m, x, 8 * g : 8 * g + 8, :] = mass
                return tuple(nexts)

            first = []
            for g in groups:
                first += sum((plane(3 * m + c, 0, g) for c in range(3)), ())
            lax.fori_loop(0, TX, body, tuple(first))
        return 0

    lax.fori_loop(0, 2, element_pass, 0)

    for wait in face_waits:
        wait()
    for o in BELOW:
        clear(from_hi, -2 * o[0] - o[1], jnp.logical_not(there(opposite(o))))
    for o in SIDES:
        clear(from_side, -2 * o[0] - o[1], jnp.logical_not(there(opposite(o))))
    below_last = lax.broadcasted_iota(jnp.int32, (8, 128), 0) < 7
    last_group, last_plane = lax.rem(lane, 4) == 3, lax.rem(lane, 64) >= 60

    def next_y(own, halo):
        own, halo = pltpu.roll(own, 7, 0), pltpu.roll(halo, 7, 0)
        over = jnp.where(last_group, pltpu.roll(halo, 3, 1), pltpu.roll(own, 127, 1))
        return jnp.where(below_last, own, over)

    def next_x(own, halo):
        return jnp.where(last_plane, pltpu.roll(halo, 60, 1), pltpu.roll(own, 124, 1))

    now, later = (), ()
    for c in range(3):
        sides = []
        for own, side in ((face[1, c], from_side), (from_hi[0, c], from_hi)):
            own_y, x_halo = next_y(own, side[1, c]), side[2, c]
            x_halo_y = next_y(x_halo, side[3, c])
            sides.append((own, own_y, next_x(own, x_halo), next_x(own_y, x_halo_y)))
        (v00, v01, v10, v11), (w00, w01, w10, w11) = sides
        now += across(v00, v01, w00, w01)
        later += across(v10, v11, w10, w11)
    edge[0], edge[1] = energies(now, later)
    last = lane >= 127

    top_t = math.tanh(4.0)
    merge_z(0, z_waits[0])
    eigs = [eig[m] for m in range(2)]

    def project(xb, acc):
        acc = list(acc)
        for i in range(4):
            x = 4 * xb + i
            xpos = mx * TX + x
            x1 = inside(xpos - 1, cx * TX) + inside(xpos + 1, cx * TX)
            x2 = inside(xpos - 2, cx * TX) + inside(xpos + 2, cx * TX)
            for g in range(4):
                rows = slice(8 * g, 8 * g + 8)
                inverse = 1.0 / (wparts[0, g] + x1 * wparts[1, g] + x2 * wparts[2, g])
                t = jnp.tanh(8.0 * ((fz[x, rows, :] + from_z(0, xb, i, g)) * inverse - 0.5))
                rho = (top_t + t) * (0.5 / top_t)
                slope = (1.0 - t * t) * inverse * (4.0 / top_t)
                cubic = (3.0 * (1.0 - 0.001)) * (rho * rho)
                for m in range(2):
                    turn = lax.rem(255 - (64 * m + 4 * x + g), 128)
                    mass = jnp.where(last, pltpu.roll(edge[1], turn, 1), mass_terms[m, x, rows, :])
                    stiff = jnp.where(last, pltpu.roll(edge[0], turn, 1), stiffs[m, x, rows, :])
                    acc[m] = acc[m] + rho * mass
                    gp[m, x + 2, 8 + 8 * g : 16 + 8 * g, :] = (
                        cubic * stiff - eigs[m] * mass
                    ) * slope
        return tuple(acc)

    masses = lax.fori_loop(0, 4, project, (zero, zero))
    for m in range(2):
        a_in[a_slot, m : m + 1, :] = jnp.sum(masses[m], axis=0, keepdims=True)

    def spread_sum(ref, count, slot, device, sem):
        def start(k, _):
            @pl.when(k != slot)
            def _():
                remote(ref.at[slot], ref.at[slot], sem, device(k)).start()

            return 0

        lax.fori_loop(0, count, start, 0)
        return remote(ref.at[pl.ds(0, count - 1)], ref.at[pl.ds(0, count - 1)], sem, me)

    a_copies = spread_sum(a_in, a_count, a_slot, a_device, 29)
    flats = send_flats(gp, gp, (slice(None),), (2, 8), 15)

    for wait in flats:
        wait()
    clear_halo(gp, (slice(None),))
    stores = []
    for m in range(2):

        def put_grad(x, g, value, m=m):
            outs[m, x, 8 * g : 8 * g + 8, :] = value

        sweep(lambda p, a, b, m=m: gp[m, p, a:b, :], put_grad, z_out.at[1 + m])
        z_waits.append(send_z(1 + m))

    a_copies.wait_recv()
    b_in[b_slot] = jnp.sum(a_in[...], axis=0)
    b_copies = spread_sum(b_in, b_count, b_slot, b_device, 30)

    for m in range(2):
        merge_z(1 + m, z_waits[1 + m])

        def finish(xb, _, m=m):
            for i in range(4):
                for g in range(4):
                    rows = slice(8 * g, 8 * g + 8)
                    outs[m, 4 * xb + i, rows, :] = outs[m, 4 * xb + i, rows, :] + from_z(
                        1 + m, xb, i, g
                    )
            return 0

        lax.fori_loop(0, 4, finish, 0)
        store = pltpu.make_async_copy(outs.at[m], raw_ref.at[m], out_sem.at[m])
        store.start()
        stores.append(store)

    b_copies.wait_recv()
    total = jnp.sum(jnp.sum(b_in[...], axis=0), axis=1, keepdims=True)
    scale_ref[...] = jnp.broadcast_to(count / total, (2, 128))

    for wait in sent:
        wait()
    a_copies.wait_send()
    b_copies.wait_send()
    for store in stores:
        store.wait()


def per_device(sizes, design, modes, eigenvalues):
    cx, cy, cz = sizes
    a_count, b_count = (cx // 2) * cz, 2 * cy
    dma = pltpu.SemaphoreType.DMA

    def vmem(*shape):
        return pltpu.VMEM(shape, F32)

    raw, scale = pl.pallas_call(
        lambda *refs: kernel(sizes, *refs),
        out_shape=(
            jax.ShapeDtypeStruct((2, TX, TY, TZ), F32),
            jax.ShapeDtypeStruct((2, 128), F32),
        ),
        in_specs=[pl.BlockSpec(memory_space=pl.ANY)] * 3,
        out_specs=(
            pl.BlockSpec(memory_space=pl.ANY),
            pl.BlockSpec(memory_space=pltpu.VMEM),
        ),
        scratch_shapes=[
            vmem(TX + 4, TY + 16, TZ),
            vmem(6, TX + 1, TY + 8, TZ),
            vmem(6, TX + 1, TY + 8, TZ),
            vmem(2, 3, 8, 128),
            vmem(4, 3, 8, 128),
            vmem(4, 3, 8, 128),
            vmem(2, 8, 128),
            vmem(3, 4, 8, 128),
            vmem(TX, TY, TZ),
            vmem(2, TX, TY, TZ),
            vmem(2, TX, TY, TZ),
            vmem(2, TX + 4, TY + 16, TZ),
            vmem(2, TX, TY, TZ),
            vmem(3, 2, 8, 128),
            vmem(3, 2, 8, 128),
            vmem(3, 2, 8, 128),
            vmem(a_count, 2, 128),
            vmem(b_count, 2, 128),
            pltpu.SMEM((2,), F32),
            dma((8,)),
            dma((2,)),
            dma((34,)),
            dma((34,)),
        ],
        compiler_params=pltpu.CompilerParams(
            collective_id=0, has_side_effects=True, vmem_limit_bytes=62 * 1024 * 1024
        ),
    )(design, modes.reshape(6, TX, TY, TZ), eigenvalues)
    return raw * scale[:, :1, None, None]


def solution(mesh):
    sizes = tuple(mesh.shape[a] for a in AXES)
    return jax.shard_map(
        lambda design, modes, eigenvalues: per_device(sizes, design, modes, eigenvalues),
        mesh=mesh,
        in_specs=(P("gx", "gy", "gz"), P(None, None, "gx", "gy", "gz"), P()),
        out_specs=P(None, "gx", "gy", "gz"),
        check_vma=False,
    )
```

```python
import functools
import itertools
import math

import jax
import jax.numpy as jnp
from jax import lax
from jax.experimental import pallas as pl
from jax.experimental.pallas import tpu as pltpu
from jax.sharding import PartitionSpec as P

AXES = ("gx", "gy", "gz")
MESH = pl.DeviceIdType.MESH
TX, TY, TZ = 16, 32, 128
FLAT = [o for o in itertools.product((-1, 0, 1), (-1, 0, 1), (0,)) if o != (0, 0, 0)]
SIDES = [(-1, 0, 0), (0, -1, 0), (-1, -1, 0)]
BELOW = [(0, 0, -1), (0, -1, -1), (-1, 0, -1), (-1, -1, -1)]
F32 = jnp.float32


def weight(i, j, k):
    return max(0.0, 3.0 - math.sqrt(i * i + j * j + k * k))


X_SPAN = {-1: (0, TX + 2, 2), 0: (0, 2, TX), 1: (TX - 2, 0, 2)}
Y_SPAN = {-1: (0, TY + 8, 2), 0: (0, 8, TY), 1: (TY - 2, 6, 2)}


def combine(values, weights):
    total = None
    for value, w in zip(values, weights):
        if w == 0.0:
            continue
        total = w * value if total is None else total + w * value
    return total


def loop(n, body, init, by=1):
    def block(q, carry):
        for i in range(by):
            carry = body(q * by + i, carry)
        return carry

    return block(0, init) if by == n else lax.fori_loop(0, n // by, block, init)


def kernel(
    sizes,
    design_ref,
    modes_ref,
    eig_ref,
    raw_ref,
    scale_ref,
    dp,
    mb,
    mz,
    face,
    from_hi,
    from_side,
    edge,
    wparts,
    fz,
    stiffs,
    mass_terms,
    gp,
    outs,
    z_out,
    z_up,
    z_down,
    a_in,
    b_in,
    eig,
    local_sem,
    out_sem,
    send_sem,
    recv_sem,
):
    cx, cy, cz = sizes
    count = float(cx * TX * cy * TY * cz * TZ)
    me = tuple(lax.axis_index(a) for a in AXES)
    mx, my, mzi = me

    def near(o):
        return tuple(m + d if d else m for m, d in zip(me, o))

    def there(o):
        ok = None
        for m, d, size in zip(me, o, sizes):
            if d:
                here = m > 0 if d < 0 else m < size - 1
                ok = here if ok is None else ok & here
        return ok

    def opposite(o):
        return tuple(-d for d in o)

    a_count, b_count = (cx // 2) * cz, 2 * cy
    a_slot = (mx // 2) * cz + mzi
    b_slot = lax.rem(mx, 2) * cy + my

    def a_device(slot):
        return ((slot // cz) * 2 + lax.rem(mx, 2), my, lax.rem(slot, cz))

    def b_device(slot):
        return ((mx // 2) * 2 + slot // cy, lax.rem(slot, cy), mzi)

    barrier = pltpu.get_barrier_semaphore()

    def greet(device):
        pl.semaphore_signal(barrier, inc=1, device_id=device, device_id_type=MESH)

    def greet_a(k, _):
        greet(a_device(lax.rem(a_slot + k, a_count)))
        return 0

    def greet_b(k, _):
        greet(b_device(lax.rem(b_slot + k, b_count)))
        return 0

    lax.fori_loop(1, a_count, greet_a, 0)
    lax.fori_loop(1, b_count, greet_b, 0)

    heard = a_count - 1 + b_count - 1
    for o in FLAT + [(0, 0, 1), (0, 0, -1)] + BELOW[1:]:
        heard = heard + there(o).astype(jnp.int32)
    for o in FLAT + [(0, 0, 1), (0, 0, -1)] + [opposite(o) for o in BELOW[1:]]:

        @pl.when(there(o))
        def _(o=o):
            greet(near(o))

    loads = [
        pltpu.make_async_copy(design_ref, dp.at[pl.ds(2, TX), pl.ds(8, TY)], local_sem.at[0])
    ]
    for c in range(6):
        loads.append(
            pltpu.make_async_copy(
                modes_ref.at[c], mb.at[c, pl.ds(0, TX), pl.ds(0, TY)], local_sem.at[1 + c]
            )
        )
    loads.append(pltpu.make_async_copy(eig_ref, eig, local_sem.at[7]))
    for load in loads:
        load.start()

    lane = lax.broadcasted_iota(jnp.int32, (8, 128), 1)
    quad = lax.shift_right_logical(lax.rem(lane + 2, 128), 2)
    first_two, last_two = lane < 2, lane >= 126
    zero = jnp.zeros((8, 128), F32)

    pl.semaphore_wait(barrier, heard)

    sent = []

    def remote(src, dst, sem, device):
        return pltpu.make_async_remote_copy(
            src_ref=src,
            dst_ref=dst,
            send_sem=send_sem.at[sem],
            recv_sem=recv_sem.at[sem],
            device_id=device,
            device_id_type=MESH,
        )

    def send(o, src, dst, sem):
        @pl.when(there(o))
        def _():
            remote(src, dst, sem, near(o)).start()

        def sent_all():
            @pl.when(there(o))
            def _():
                remote(src, dst, sem, near(o)).wait_send()

        def received():
            @pl.when(there(opposite(o)))
            def _():
                remote(src, dst, sem, near(o)).wait_recv()

        sent.append(sent_all)
        return received

    def send_flats(src, dst, lead, shift, sem):
        waits = []
        for i, o in enumerate(FLAT):
            (xs, xd, xn), (ys, yd, yn) = X_SPAN[o[0]], Y_SPAN[o[1]]
            waits.append(
                send(
                    o,
                    src.at[lead + (pl.ds(xs + shift[0], xn), pl.ds(ys + shift[1], yn))],
                    dst.at[lead + (pl.ds(xd, xn), pl.ds(yd, yn))],
                    sem + i,
                )
            )
        return waits

    loads[0].wait()
    design_waits = send_flats(dp, dp, (), (2, 8), 0)
    mode_waits = []
    for i, o in enumerate(SIDES):
        dx, dy, _ = o
        xs = pl.ds(0, 1) if dx else pl.ds(0, TX)
        xd = pl.ds(TX, 1) if dx else pl.ds(0, TX)
        ys = pl.ds(0, 1) if dy else pl.ds(0, TY)
        yd = pl.ds(TY, 1) if dy else pl.ds(0, TY)
        mode_waits.append(send(o, modes_ref.at[:, xs, ys], mb.at[:, xd, yd], 8 + i))

    def inside(cell, total):
        return ((cell >= 0) & (cell < total)).astype(F32)

    zpos = mzi * TZ + lane
    z1 = inside(zpos - 1, cz * TZ) + inside(zpos + 1, cz * TZ)
    z2 = inside(zpos - 2, cz * TZ) + inside(zpos + 2, cz * TZ)
    for g in range(4):
        ypos = my * TY + 8 * g + lax.broadcasted_iota(jnp.int32, (8, 128), 0)
        y1 = inside(ypos - 1, cy * TY) + inside(ypos + 1, cy * TY)
        y2 = inside(ypos - 2, cy * TY) + inside(ypos + 2, cy * TY)
        for i in range(3):
            rows = [
                weight(i, j, 0) + weight(i, j, 1) * z1 + weight(i, j, 2) * z2 for j in range(3)
            ]
            wparts[i, g] = rows[0] + y1 * rows[1] + y2 * rows[2]

    for load in loads[1:]:
        load.wait()

    def pack_modes(x, carry):
        first, final = (list(v) for v in carry)
        for c in range(6):
            for g in range(4):
                k = (c // 3) * 64 + 4 * x + g
                r = pltpu.roll(mb[c, x, 8 * g : 8 * g + 8, :], k, 1)
                first[c % 3] = jnp.where(lane == k, r, first[c % 3])
                final[c % 3] = jnp.where(lane == (k + 127) % 128, r, final[c % 3])
        return tuple(first), tuple(final)

    first, final = loop(TX, pack_modes, ((zero,) * 3, (zero,) * 3), TX)
    for c in range(3):
        face[0, c] = first[c]
        face[1, c] = pltpu.roll(final[c], 1, 1)

    face_waits = []
    for i, o in enumerate(BELOW):
        face_waits.append(send(o, face.at[0], from_hi.at[-2 * o[0] - o[1]], 11 + i))
    for i, o in enumerate(SIDES):
        face_waits.append(send(o, face.at[1], from_side.at[-2 * o[0] - o[1]], 31 + i))

    def shift_modes(x, _):
        for c in range(6):
            for g in range(4):
                rows = slice(8 * g, 8 * g + 8)
                mz[c, x, rows, :] = pltpu.roll(mb[c, x, rows, :], 127, 1)
        return 0

    loop(TX, shift_modes, 0, 4)

    def clear(ref, index, cond):
        @pl.when(cond)
        def _():
            ref[index] = jnp.zeros_like(ref[index])

    def clear_halo(ref, lead):
        clear(ref, lead + (slice(0, 2),), mx == 0)
        clear(ref, lead + (slice(TX + 2, TX + 4),), mx == cx - 1)
        clear(ref, lead + (slice(None), slice(0, 8)), my == 0)
        clear(ref, lead + (slice(None), slice(TY + 8, TY + 16)), my == cy - 1)

    order = ((0, 0), (0, 1), (1, 1), (0, 2), (1, 2), (2, 2))

    def sweep(load, put, packs):
        packs[0] = zero
        packs[1] = zero

        def body(xb, _):
            held = packs[xb // 2]
            for g in range(4):
                top = 8 + 8 * g
                a = {}
                for t in range(8):
                    p = 4 * xb + t
                    a[t, 0] = load(p, top, top + 8)
                    a[t, 1] = load(p, top - 1, top + 7) + load(p, top + 1, top + 9)
                    a[t, 2] = load(p, top - 2, top + 6) + load(p, top + 2, top + 10)
                for i in range(4):
                    b = {}
                    for j in range(3):
                        b[0, j] = a[i + 2, j]
                        b[1, j] = a[i + 1, j] + a[i + 3, j]
                        b[2, j] = a[i, j] + a[i + 4, j]
                    grouped = [b[u, v] if u == v else b[u, v] + b[v, u] for u, v in order]
                    e0, e1, e2 = (
                        combine(grouped, [weight(u, v, k) for u, v in order]) for k in range(3)
                    )
                    up, down = pltpu.roll(e1, 1, 1), pltpu.roll(e1, 127, 1)
                    up2, down2 = pltpu.roll(e2, 2, 1), pltpu.roll(e2, 126, 1)
                    out = jnp.where(lane < 1, up, jnp.where(lane >= 127, down, 0.0)) + jnp.where(
                        first_two, up2, jnp.where(last_two, down2, 0.0)
                    )
                    put(4 * xb + i, g, (e0 + ((up + down) + (up2 + down2))) - out)
                    k = lax.rem(xb, 2) * 16 + 4 * i + g
                    held = jnp.where(quad == k, pltpu.roll(out, 4 * k, 1), held)
            packs[xb // 2] = held
            return 0

        lax.fori_loop(0, 4, body, 0)

    def send_z(f):
        return (
            send((0, 0, -1), z_out.at[f], z_up.at[f], 23 + f),
            send((0, 0, 1), z_out.at[f], z_down.at[f], 26 + f),
        )

    def merge_z(f, waits):
        for wait in waits:
            wait()
        clear(z_up, f, mzi == cz - 1)
        clear(z_down, f, mzi == 0)
        for h in range(2):
            z_up[f, h] = jnp.where(lax.rem(lane, 4) >= 2, z_up[f, h], z_down[f, h])

    def from_z(f, xb, i, g):
        k = lax.rem(xb, 2) * 16 + 4 * i + g
        r = pltpu.roll(z_up[f, xb // 2], lax.rem(128 - 4 * k, 128), 1)
        return jnp.where(first_two | last_two, r, 0.0)

    factor = 1.0 / (1.3 * 0.4)
    lam, mu = 0.3 * factor, 0.2 * factor

    def across(v0, v1, w0, w1):
        vs, vd, ws, wd = v0 + v1, v1 - v0, w0 + w1, w1 - w0
        return vs + ws, ws - vs, vd + wd, wd - vd

    def plane(c, x, g):
        a, b = 8 * g, 8 * g + 8
        v0, v1 = mb[c, x, a:b, :], mb[c, x, a + 1 : b + 1, :]
        return across(v0, v1, mz[c, x, a:b, :], mz[c, x, a + 1 : b + 1, :])

    def energies(now, later):
        a = {}
        for c in range(3):
            for q, (j, k) in enumerate(((0, 0), (0, 1), (1, 0), (1, 1))):
                a[c, 0, j, k] = now[4 * c + q] + later[4 * c + q]
                a[c, 1, j, k] = later[4 * c + q] - now[4 * c + q]
        s = {key: v * v for key, v in a.items()}

        def sq(v):
            return v * v

        q0 = s[0, 0, 0, 0] + s[1, 0, 0, 0] + s[2, 0, 0, 0]
        axial = s[0, 1, 0, 0] + s[1, 0, 1, 0] + s[2, 0, 0, 1]
        slide = (
            (s[0, 0, 1, 0] + s[0, 0, 0, 1])
            + (s[1, 1, 0, 0] + s[1, 0, 0, 1])
            + (s[2, 1, 0, 0] + s[2, 0, 1, 0])
        )
        q1 = axial + slide
        bend = (
            (s[0, 1, 1, 0] + s[0, 1, 0, 1])
            + (s[1, 1, 1, 0] + s[1, 0, 1, 1])
            + (s[2, 1, 0, 1] + s[2, 0, 1, 1])
        )
        twist = s[0, 0, 1, 1] + s[1, 1, 0, 1] + s[2, 1, 1, 0]
        q2 = bend + twist
        q3 = s[0, 1, 1, 1] + s[1, 1, 1, 1] + s[2, 1, 1, 1]
        mass = (1 / 64) * q0 + (1 / 192) * q1 + ((1 / 576) * q2 + (1 / 1728) * q3)
        trace = sq(a[0, 1, 0, 0] + a[1, 0, 1, 0] + a[2, 0, 0, 1])
        cross = (
            a[0, 0, 1, 0] * a[1, 1, 0, 0]
            + a[1, 0, 0, 1] * a[2, 0, 1, 0]
            + a[0, 0, 0, 1] * a[2, 1, 0, 0]
        )
        cross_1 = (
            a[0, 1, 1, 0] * a[2, 0, 1, 1]
            + a[0, 1, 0, 1] * a[1, 0, 1, 1]
            + a[1, 1, 1, 0] * a[2, 1, 0, 1]
        )
        shear_1 = sq(a[0, 0, 1, 1] + a[1, 1, 0, 1] + a[2, 1, 1, 0]) + twist
        stiff = (
            ((lam / 16) * trace + (mu / 8) * (axial + cross))
            + ((mu / 16) * slide + (lam / 24) * cross_1)
            + ((mu / 16 + lam / 48) * bend + (mu / 48) * shear_1)
            + ((lam + 4 * mu) / 144) * q3
        )
        return stiff, mass

    def element_pass(spans, m, _):
        for pairs, x_from, x_to in spans:
            groups = (2 * pairs, 2 * pairs + 1)

            def body(x, held):
                nexts = []
                for i, g in enumerate(groups):
                    later = sum((plane(3 * m + c, x + 1, g) for c in range(3)), ())
                    nexts += later
                    stiff, mass = energies(held[12 * i : 12 * i + 12], later)
                    stiffs[m, x, 8 * g : 8 * g + 8, :] = stiff
                    mass_terms[m, x, 8 * g : 8 * g + 8, :] = mass
                return tuple(nexts)

            first = []
            for g in groups:
                first += sum((plane(3 * m + c, x_from, g) for c in range(3)), ())
            lax.fori_loop(x_from, x_to, body, tuple(first))
        return 0

    lax.fori_loop(0, 2, functools.partial(element_pass, ((0, 0, TX - 1),)), 0)

    for wait in design_waits:
        wait()
    clear_halo(dp, ())

    def put_design(x, g, value):
        fz[x, 8 * g : 8 * g + 8, :] = value

    sweep(lambda p, a, b: dp[p, a:b, :], put_design, z_out.at[0])
    z_waits = [send_z(0)]

    for wait in mode_waits:
        wait()
    clear(mb, (slice(None), TX), mx == cx - 1)
    clear(mb, (slice(None), slice(None), slice(TY, TY + 8)), my == cy - 1)

    def shift_halo(c, _):
        for x in range(TX + 1):
            mz[c, x, TY : TY + 8, :] = pltpu.roll(mb[c, x, TY : TY + 8, :], 127, 1)
        for g in range(4):
            rows = slice(8 * g, 8 * g + 8)
            mz[c, TX, rows, :] = pltpu.roll(mb[c, TX, rows, :], 127, 1)
        return 0

    loop(6, shift_halo, 0, 2)

    lax.fori_loop(0, 2, functools.partial(element_pass, ((0, TX - 1, TX), (1, 0, TX))), 0)

    for wait in face_waits:
        wait()
    for o in BELOW:
        clear(from_hi, -2 * o[0] - o[1], jnp.logical_not(there(opposite(o))))
    for o in SIDES:
        clear(from_side, -2 * o[0] - o[1], jnp.logical_not(there(opposite(o))))
    below_last = lax.broadcasted_iota(jnp.int32, (8, 128), 0) < 7
    last_group, last_plane = lax.rem(lane, 4) == 3, lax.rem(lane, 64) >= 60

    def next_y(own, halo):
        own, halo = pltpu.roll(own, 7, 0), pltpu.roll(halo, 7, 0)
        over = jnp.where(last_group, pltpu.roll(halo, 3, 1), pltpu.roll(own, 127, 1))
        return jnp.where(below_last, own, over)

    def next_x(own, halo):
        return jnp.where(last_plane, pltpu.roll(halo, 60, 1), pltpu.roll(own, 124, 1))

    now, later = (), ()
    for c in range(3):
        sides = []
        for own, side in ((face[1, c], from_side), (from_hi[0, c], from_hi)):
            own_y, x_halo = next_y(own, side[1, c]), side[2, c]
            x_halo_y = next_y(x_halo, side[3, c])
            sides.append((own, own_y, next_x(own, x_halo), next_x(own_y, x_halo_y)))
        (v00, v01, v10, v11), (w00, w01, w10, w11) = sides
        now += across(v00, v01, w00, w01)
        later += across(v10, v11, w10, w11)
    edge[0], edge[1] = energies(now, later)
    last = lane >= 127

    top_t = math.tanh(4.0)
    merge_z(0, z_waits[0])
    eigs = [eig[m] for m in range(2)]

    def project(xb, acc):
        acc = list(acc)
        for i in range(4):
            x = 4 * xb + i
            xpos = mx * TX + x
            x1 = inside(xpos - 1, cx * TX) + inside(xpos + 1, cx * TX)
            x2 = inside(xpos - 2, cx * TX) + inside(xpos + 2, cx * TX)
            for g in range(4):
                rows = slice(8 * g, 8 * g + 8)
                inverse = 1.0 / (wparts[0, g] + x1 * wparts[1, g] + x2 * wparts[2, g])
                t = jnp.tanh(8.0 * ((fz[x, rows, :] + from_z(0, xb, i, g)) * inverse - 0.5))
                rho = (top_t + t) * (0.5 / top_t)
                slope = (1.0 - t * t) * inverse * (4.0 / top_t)
                cubic = (3.0 * (1.0 - 0.001)) * (rho * rho)
                for m in range(2):
                    turn = lax.rem(255 - (64 * m + 4 * x + g), 128)
                    mass = jnp.where(last, pltpu.roll(edge[1], turn, 1), mass_terms[m, x, rows, :])
                    stiff = jnp.where(last, pltpu.roll(edge[0], turn, 1), stiffs[m, x, rows, :])
                    acc[m] = acc[m] + rho * mass
                    gp[m, x + 2, 8 + 8 * g : 16 + 8 * g, :] = (
                        cubic * stiff - eigs[m] * mass
                    ) * slope
        return tuple(acc)

    masses = lax.fori_loop(0, 4, project, (zero, zero))
    for m in range(2):
        a_in[a_slot, m : m + 1, :] = jnp.sum(masses[m], axis=0, keepdims=True)

    def spread_sum(ref, count, slot, device, sem):
        def start(k, _):
            @pl.when(k != slot)
            def _():
                remote(ref.at[slot], ref.at[slot], sem, device(k)).start()

            return 0

        lax.fori_loop(0, count, start, 0)
        return remote(ref.at[pl.ds(0, count - 1)], ref.at[pl.ds(0, count - 1)], sem, me)

    a_copies = spread_sum(a_in, a_count, a_slot, a_device, 29)
    flats = send_flats(gp, gp, (slice(None),), (2, 8), 15)

    for wait in flats:
        wait()
    clear_halo(gp, (slice(None),))
    stores = []
    for m in range(2):

        def put_grad(x, g, value, m=m):
            outs[m, x, 8 * g : 8 * g + 8, :] = value

        sweep(lambda p, a, b, m=m: gp[m, p, a:b, :], put_grad, z_out.at[1 + m])
        z_waits.append(send_z(1 + m))

    a_copies.wait_recv()
    b_in[b_slot] = jnp.sum(a_in[...], axis=0)
    b_copies = spread_sum(b_in, b_count, b_slot, b_device, 30)

    for m in range(2):
        merge_z(1 + m, z_waits[1 + m])

        def finish(xb, _, m=m):
            for i in range(4):
                for g in range(4):
                    rows = slice(8 * g, 8 * g + 8)
                    outs[m, 4 * xb + i, rows, :] = outs[m, 4 * xb + i, rows, :] + from_z(
                        1 + m, xb, i, g
                    )
            return 0

        lax.fori_loop(0, 4, finish, 0)
        store = pltpu.make_async_copy(outs.at[m], raw_ref.at[m], out_sem.at[m])
        store.start()
        stores.append(store)

    b_copies.wait_recv()
    total = jnp.sum(jnp.sum(b_in[...], axis=0), axis=1, keepdims=True)
    scale_ref[...] = jnp.broadcast_to(count / total, (2, 128))

    for wait in sent:
        wait()
    a_copies.wait_send()
    b_copies.wait_send()
    for store in stores:
        store.wait()


def per_device(sizes, design, modes, eigenvalues):
    cx, cy, cz = sizes
    a_count, b_count = (cx // 2) * cz, 2 * cy
    dma = pltpu.SemaphoreType.DMA

    def vmem(*shape):
        return pltpu.VMEM(shape, F32)

    arguments = (design, modes.reshape(6, TX, TY, TZ), eigenvalues)
    raw, scale = pl.pallas_call(
        lambda *refs: kernel(sizes, *refs),
        out_shape=(
            jax.ShapeDtypeStruct((2, TX, TY, TZ), F32),
            jax.ShapeDtypeStruct((2, 128), F32),
        ),
        in_specs=[pl.BlockSpec(memory_space=pl.ANY)] * 3,
        out_specs=(
            pl.BlockSpec(memory_space=pl.ANY),
            pl.BlockSpec(memory_space=pltpu.VMEM),
        ),
        scratch_shapes=[
            vmem(TX + 4, TY + 16, TZ),
            vmem(6, TX + 1, TY + 8, TZ),
            vmem(6, TX + 1, TY + 8, TZ),
            vmem(2, 3, 8, 128),
            vmem(4, 3, 8, 128),
            vmem(4, 3, 8, 128),
            vmem(2, 8, 128),
            vmem(3, 4, 8, 128),
            vmem(TX, TY, TZ),
            vmem(2, TX, TY, TZ),
            vmem(2, TX, TY, TZ),
            vmem(2, TX + 4, TY + 16, TZ),
            vmem(2, TX, TY, TZ),
            vmem(3, 2, 8, 128),
            vmem(3, 2, 8, 128),
            vmem(3, 2, 8, 128),
            vmem(a_count, 2, 128),
            vmem(b_count, 2, 128),
            pltpu.SMEM((2,), F32),
            dma((8,)),
            dma((2,)),
            dma((34,)),
            dma((34,)),
        ],
        compiler_params=pltpu.CompilerParams(
            collective_id=0, has_side_effects=True, vmem_limit_bytes=24 * 1024 * 1024
        ),
    )(*(pltpu.with_memory_space_constraint(v, pltpu.HBM) for v in arguments))
    return raw * scale[:, None, None, :]


def solution(mesh):
    sizes = tuple(mesh.shape[a] for a in AXES)
    return jax.shard_map(
        lambda design, modes, eigenvalues: per_device(sizes, design, modes, eigenvalues),
        mesh=mesh,
        in_specs=(P("gx", "gy", "gz"), P(None, None, "gx", "gy", "gz"), P()),
        out_specs=P(None, "gx", "gy", "gz"),
        check_vma=False,
    )
```

```python
import functools
import itertools
import math

import jax
import jax.numpy as jnp
from jax import lax
from jax.experimental import pallas as pl
from jax.experimental.pallas import tpu as pltpu
from jax.sharding import PartitionSpec as P

AXES = ("gx", "gy", "gz")
MESH = pl.DeviceIdType.MESH
TX, TY, TZ = 16, 32, 128
FLAT = [o for o in itertools.product((-1, 0, 1), (-1, 0, 1), (0,)) if o != (0, 0, 0)]
SIDES = [(-1, 0, 0), (0, -1, 0), (-1, -1, 0)]
BELOW = [(0, 0, -1), (0, -1, -1), (-1, 0, -1), (-1, -1, -1)]
F32 = jnp.float32


def weight(i, j, k):
    return max(0.0, 3.0 - math.sqrt(i * i + j * j + k * k))


X_SPAN = {-1: (0, TX + 2, 2), 0: (0, 2, TX), 1: (TX - 2, 0, 2)}
Y_SPAN = {-1: (0, TY + 8, 2), 0: (0, 8, TY), 1: (TY - 2, 6, 2)}


def combine(values, weights):
    total = None
    for value, w in zip(values, weights):
        if w == 0.0:
            continue
        total = w * value if total is None else total + w * value
    return total


def loop(n, body, init, by=1):
    def block(q, carry):
        for i in range(by):
            carry = body(q * by + i, carry)
        return carry

    return block(0, init) if by == n else lax.fori_loop(0, n // by, block, init)


def kernel(
    sizes,
    design_ref,
    modes_ref,
    eig_ref,
    raw_ref,
    scale_ref,
    dp,
    mb,
    mz,
    face,
    from_hi,
    from_side,
    edge,
    wparts,
    fz,
    slopes,
    cubics,
    stiffs,
    mass_terms,
    gp,
    outs,
    z_out,
    z_up,
    z_down,
    a_in,
    b_in,
    eig,
    local_sem,
    out_sem,
    send_sem,
    recv_sem,
):
    cx, cy, cz = sizes
    count = float(cx * TX * cy * TY * cz * TZ)
    me = tuple(lax.axis_index(a) for a in AXES)
    mx, my, mzi = me

    def near(o):
        return tuple(m + d if d else m for m, d in zip(me, o))

    def there(o):
        ok = None
        for m, d, size in zip(me, o, sizes):
            if d:
                here = m > 0 if d < 0 else m < size - 1
                ok = here if ok is None else ok & here
        return ok

    def opposite(o):
        return tuple(-d for d in o)

    a_count, b_count = (cx // 2) * cz, 2 * cy
    a_slot = (mx // 2) * cz + mzi
    b_slot = lax.rem(mx, 2) * cy + my

    def a_device(slot):
        return ((slot // cz) * 2 + lax.rem(mx, 2), my, lax.rem(slot, cz))

    def b_device(slot):
        return ((mx // 2) * 2 + slot // cy, lax.rem(slot, cy), mzi)

    barrier = pltpu.get_barrier_semaphore()

    def greet(device):
        pl.semaphore_signal(barrier, inc=1, device_id=device, device_id_type=MESH)

    def greet_a(k, _):
        greet(a_device(lax.rem(a_slot + k, a_count)))
        return 0

    def greet_b(k, _):
        greet(b_device(lax.rem(b_slot + k, b_count)))
        return 0

    for k in range(1, a_count):
        greet_a(k, 0)
    for k in range(1, b_count):
        greet_b(k, 0)

    heard = a_count - 1 + b_count - 1
    for o in FLAT + [(0, 0, 1), (0, 0, -1)] + BELOW[1:]:
        heard = heard + there(o).astype(jnp.int32)
    for o in FLAT + [(0, 0, 1), (0, 0, -1)] + [opposite(o) for o in BELOW[1:]]:

        @pl.when(there(o))
        def _(o=o):
            greet(near(o))

    loads = [
        pltpu.make_async_copy(design_ref, dp.at[pl.ds(2, TX), pl.ds(8, TY)], local_sem.at[0])
    ]
    for c in range(6):
        loads.append(
            pltpu.make_async_copy(
                modes_ref.at[c], mb.at[c, pl.ds(0, TX), pl.ds(0, TY)], local_sem.at[1 + c]
            )
        )
    loads.append(pltpu.make_async_copy(eig_ref, eig, local_sem.at[7]))
    for load in loads:
        load.start()

    lane = lax.broadcasted_iota(jnp.int32, (8, 128), 1)
    quad = lax.shift_right_logical(lax.rem(lane + 2, 128), 2)
    first_two, last_two = lane < 2, lane >= 126
    zero = jnp.zeros((8, 128), F32)

    pl.semaphore_wait(barrier, heard)

    sent = []

    def remote(src, dst, sem, device):
        return pltpu.make_async_remote_copy(
            src_ref=src,
            dst_ref=dst,
            send_sem=send_sem.at[sem],
            recv_sem=recv_sem.at[sem],
            device_id=device,
            device_id_type=MESH,
        )

    def send(o, src, dst, sem):
        @pl.when(there(o))
        def _():
            remote(src, dst, sem, near(o)).start()

        def sent_all():
            @pl.when(there(o))
            def _():
                remote(src, dst, sem, near(o)).wait_send()

        def received():
            @pl.when(there(opposite(o)))
            def _():
                remote(src, dst, sem, near(o)).wait_recv()

        sent.append(sent_all)
        return received

    def send_flats(src, dst, lead, shift, sem):
        waits = []
        for i, o in enumerate(FLAT):
            (xs, xd, xn), (ys, yd, yn) = X_SPAN[o[0]], Y_SPAN[o[1]]
            waits.append(
                send(
                    o,
                    src.at[lead + (pl.ds(xs + shift[0], xn), pl.ds(ys + shift[1], yn))],
                    dst.at[lead + (pl.ds(xd, xn), pl.ds(yd, yn))],
                    sem + i,
                )
            )
        return waits

    loads[0].wait()
    design_waits = send_flats(dp, dp, (), (2, 8), 0)
    mode_waits = []
    for i, o in enumerate(SIDES):
        dx, dy, _ = o
        xs = pl.ds(0, 1) if dx else pl.ds(0, TX)
        xd = pl.ds(TX, 1) if dx else pl.ds(0, TX)
        ys = pl.ds(0, 1) if dy else pl.ds(0, TY)
        yd = pl.ds(TY, 1) if dy else pl.ds(0, TY)
        mode_waits.append(send(o, modes_ref.at[:, xs, ys], mb.at[:, xd, yd], 8 + i))

    def inside(cell, total):
        return ((cell >= 0) & (cell < total)).astype(F32)

    zpos = mzi * TZ + lane
    z1 = inside(zpos - 1, cz * TZ) + inside(zpos + 1, cz * TZ)
    z2 = inside(zpos - 2, cz * TZ) + inside(zpos + 2, cz * TZ)
    for g in range(4):
        ypos = my * TY + 8 * g + lax.broadcasted_iota(jnp.int32, (8, 128), 0)
        y1 = inside(ypos - 1, cy * TY) + inside(ypos + 1, cy * TY)
        y2 = inside(ypos - 2, cy * TY) + inside(ypos + 2, cy * TY)
        for i in range(3):
            rows = [
                weight(i, j, 0) + weight(i, j, 1) * z1 + weight(i, j, 2) * z2 for j in range(3)
            ]
            wparts[i, g] = rows[0] + y1 * rows[1] + y2 * rows[2]

    for load in loads[1:]:
        load.wait()

    def pack_modes(x, carry):
        first, final = (list(v) for v in carry)
        for c in range(6):
            for g in range(4):
                k = (c // 3) * 64 + 4 * x + g
                r = pltpu.roll(mb[c, x, 8 * g : 8 * g + 8, :], k, 1)
                first[c % 3] = jnp.where(lane == k, r, first[c % 3])
                final[c % 3] = jnp.where(lane == (k + 127) % 128, r, final[c % 3])
        return tuple(first), tuple(final)

    first, final = loop(TX, pack_modes, ((zero,) * 3, (zero,) * 3), TX)
    for c in range(3):
        face[0, c] = first[c]
        face[1, c] = pltpu.roll(final[c], 1, 1)

    face_waits = []
    for i, o in enumerate(BELOW):
        face_waits.append(send(o, face.at[0], from_hi.at[-2 * o[0] - o[1]], 11 + i))
    for i, o in enumerate(SIDES):
        face_waits.append(send(o, face.at[1], from_side.at[-2 * o[0] - o[1]], 31 + i))

    def shift_modes(x, _):
        for c in range(6):
            for g in range(4):
                rows = slice(8 * g, 8 * g + 8)
                mz[c, x, rows, :] = pltpu.roll(mb[c, x, rows, :], 127, 1)
        return 0

    loop(TX, shift_modes, 0, 4)

    def clear(ref, index, cond):
        @pl.when(cond)
        def _():
            ref[index] = jnp.zeros_like(ref[index])

    def clear_halo(ref, lead):
        clear(ref, lead + (slice(0, 2),), mx == 0)
        clear(ref, lead + (slice(TX + 2, TX + 4),), mx == cx - 1)
        clear(ref, lead + (slice(None), slice(0, 8)), my == 0)
        clear(ref, lead + (slice(None), slice(TY + 8, TY + 16)), my == cy - 1)

    order = ((0, 0), (0, 1), (1, 1), (0, 2), (1, 2), (2, 2))

    def sweep(load, put, packs):
        packs[0] = zero
        packs[1] = zero

        def body(xb, _):
            held = packs[xb // 2]
            for g in range(4):
                top = 8 + 8 * g
                a = {}
                for t in range(8):
                    p = 4 * xb + t
                    a[t, 0] = load(p, top, top + 8)
                    a[t, 1] = load(p, top - 1, top + 7) + load(p, top + 1, top + 9)
                    a[t, 2] = load(p, top - 2, top + 6) + load(p, top + 2, top + 10)
                for i in range(4):
                    b = {}
                    for j in range(3):
                        b[0, j] = a[i + 2, j]
                        b[1, j] = a[i + 1, j] + a[i + 3, j]
                        b[2, j] = a[i, j] + a[i + 4, j]
                    grouped = [b[u, v] if u == v else b[u, v] + b[v, u] for u, v in order]
                    e0, e1, e2 = (
                        combine(grouped, [weight(u, v, k) for u, v in order]) for k in range(3)
                    )
                    up, down = pltpu.roll(e1, 1, 1), pltpu.roll(e1, 127, 1)
                    up2, down2 = pltpu.roll(e2, 2, 1), pltpu.roll(e2, 126, 1)
                    out = jnp.where(lane < 1, up, jnp.where(lane >= 127, down, 0.0)) + jnp.where(
                        first_two, up2, jnp.where(last_two, down2, 0.0)
                    )
                    put(4 * xb + i, g, (e0 + ((up + down) + (up2 + down2))) - out)
                    k = lax.rem(xb, 2) * 16 + 4 * i + g
                    held = jnp.where(quad == k, pltpu.roll(out, 4 * k, 1), held)
            packs[xb // 2] = held
            return 0

        lax.fori_loop(0, 4, body, 0)

    def send_z(f):
        return (
            send((0, 0, -1), z_out.at[f], z_up.at[f], 23 + f),
            send((0, 0, 1), z_out.at[f], z_down.at[f], 26 + f),
        )

    def merge_z(f, waits):
        for wait in waits:
            wait()
        clear(z_up, f, mzi == cz - 1)
        clear(z_down, f, mzi == 0)
        for h in range(2):
            z_up[f, h] = jnp.where(lax.rem(lane, 4) >= 2, z_up[f, h], z_down[f, h])

    def from_z(f, xb, i, g):
        k = lax.rem(xb, 2) * 16 + 4 * i + g
        r = pltpu.roll(z_up[f, xb // 2], lax.rem(128 - 4 * k, 128), 1)
        return jnp.where(first_two | last_two, r, 0.0)

    factor = 1.0 / (1.3 * 0.4)
    lam, mu = 0.3 * factor, 0.2 * factor

    def across(v0, v1, w0, w1):
        vs, vd, ws, wd = v0 + v1, v1 - v0, w0 + w1, w1 - w0
        return vs + ws, ws - vs, vd + wd, wd - vd

    def plane(c, x, g):
        a, b = 8 * g, 8 * g + 8
        v0, v1 = mb[c, x, a:b, :], mb[c, x, a + 1 : b + 1, :]
        return across(v0, v1, mz[c, x, a:b, :], mz[c, x, a + 1 : b + 1, :])

    def energies(now, later):
        a = {}
        for c in range(3):
            for q, (j, k) in enumerate(((0, 0), (0, 1), (1, 0), (1, 1))):
                a[c, 0, j, k] = now[4 * c + q] + later[4 * c + q]
                a[c, 1, j, k] = later[4 * c + q] - now[4 * c + q]
        s = {key: v * v for key, v in a.items()}

        def sq(v):
            return v * v

        q0 = s[0, 0, 0, 0] + s[1, 0, 0, 0] + s[2, 0, 0, 0]
        axial = s[0, 1, 0, 0] + s[1, 0, 1, 0] + s[2, 0, 0, 1]
        slide = (
            (s[0, 0, 1, 0] + s[0, 0, 0, 1])
            + (s[1, 1, 0, 0] + s[1, 0, 0, 1])
            + (s[2, 1, 0, 0] + s[2, 0, 1, 0])
        )
        q1 = axial + slide
        bend = (
            (s[0, 1, 1, 0] + s[0, 1, 0, 1])
            + (s[1, 1, 1, 0] + s[1, 0, 1, 1])
            + (s[2, 1, 0, 1] + s[2, 0, 1, 1])
        )
        twist = s[0, 0, 1, 1] + s[1, 1, 0, 1] + s[2, 1, 1, 0]
        q2 = bend + twist
        q3 = s[0, 1, 1, 1] + s[1, 1, 1, 1] + s[2, 1, 1, 1]
        mass = (1 / 64) * q0 + (1 / 192) * q1 + ((1 / 576) * q2 + (1 / 1728) * q3)
        trace = sq(a[0, 1, 0, 0] + a[1, 0, 1, 0] + a[2, 0, 0, 1])
        cross = (
            a[0, 0, 1, 0] * a[1, 1, 0, 0]
            + a[1, 0, 0, 1] * a[2, 0, 1, 0]
            + a[0, 0, 0, 1] * a[2, 1, 0, 0]
        )
        cross_1 = (
            a[0, 1, 1, 0] * a[2, 0, 1, 1]
            + a[0, 1, 0, 1] * a[1, 0, 1, 1]
            + a[1, 1, 1, 0] * a[2, 1, 0, 1]
        )
        shear_1 = sq(a[0, 0, 1, 1] + a[1, 1, 0, 1] + a[2, 1, 1, 0]) + twist
        stiff = (
            ((lam / 16) * trace + (mu / 8) * (axial + cross))
            + ((mu / 16) * slide + (lam / 24) * cross_1)
            + ((mu / 16 + lam / 48) * bend + (mu / 48) * shear_1)
            + ((lam + 4 * mu) / 144) * q3
        )
        return stiff, mass

    def element_pass(spans, m, _):
        for pairs, x_from, x_to in spans:
            groups = (2 * pairs, 2 * pairs + 1)

            def body(x, held):
                nexts = []
                for i, g in enumerate(groups):
                    later = sum((plane(3 * m + c, x + 1, g) for c in range(3)), ())
                    nexts += later
                    stiff, mass = energies(held[12 * i : 12 * i + 12], later)
                    stiffs[m, x, 8 * g : 8 * g + 8, :] = stiff
                    mass_terms[m, x, 8 * g : 8 * g + 8, :] = mass
                return tuple(nexts)

            first = []
            for g in groups:
                first += sum((plane(3 * m + c, x_from, g) for c in range(3)), ())
            lax.fori_loop(x_from, x_to, body, tuple(first))
        return 0

    lax.fori_loop(0, 2, functools.partial(element_pass, ((0, 0, TX - 1),)), 0)

    for wait in design_waits:
        wait()
    clear_halo(dp, ())

    def put_design(x, g, value):
        fz[x, 8 * g : 8 * g + 8, :] = value

    sweep(lambda p, a, b: dp[p, a:b, :], put_design, z_out.at[0])
    z_waits = [send_z(0)]

    for wait in mode_waits:
        wait()
    clear(mb, (slice(None), TX), mx == cx - 1)
    clear(mb, (slice(None), slice(None), slice(TY, TY + 8)), my == cy - 1)

    def shift_halo(c, _):
        for x in range(TX + 1):
            mz[c, x, TY : TY + 8, :] = pltpu.roll(mb[c, x, TY : TY + 8, :], 127, 1)
        for g in range(4):
            rows = slice(8 * g, 8 * g + 8)
            mz[c, TX, rows, :] = pltpu.roll(mb[c, TX, rows, :], 127, 1)
        return 0

    loop(6, shift_halo, 0, 2)

    lax.fori_loop(0, 2, functools.partial(element_pass, ((0, TX - 1, TX), (1, 0, TX))), 0)

    for wait in face_waits:
        wait()
    for o in BELOW:
        clear(from_hi, -2 * o[0] - o[1], jnp.logical_not(there(opposite(o))))
    for o in SIDES:
        clear(from_side, -2 * o[0] - o[1], jnp.logical_not(there(opposite(o))))
    below_last = lax.broadcasted_iota(jnp.int32, (8, 128), 0) < 7
    last_group, last_plane = lax.rem(lane, 4) == 3, lax.rem(lane, 64) >= 60

    def next_y(own, halo):
        own, halo = pltpu.roll(own, 7, 0), pltpu.roll(halo, 7, 0)
        over = jnp.where(last_group, pltpu.roll(halo, 3, 1), pltpu.roll(own, 127, 1))
        return jnp.where(below_last, own, over)

    def next_x(own, halo):
        return jnp.where(last_plane, pltpu.roll(halo, 60, 1), pltpu.roll(own, 124, 1))

    now, later = (), ()
    for c in range(3):
        sides = []
        for own, side in ((face[1, c], from_side), (from_hi[0, c], from_hi)):
            own_y, x_halo = next_y(own, side[1, c]), side[2, c]
            x_halo_y = next_y(x_halo, side[3, c])
            sides.append((own, own_y, next_x(own, x_halo), next_x(own_y, x_halo_y)))
        (v00, v01, v10, v11), (w00, w01, w10, w11) = sides
        now += across(v00, v01, w00, w01)
        later += across(v10, v11, w10, w11)
    edge[0], edge[1] = energies(now, later)
    last = lane >= 127

    def patch_last(xb, _):
        for i in range(4):
            for g in range(4):
                x, rows = 4 * xb + i, slice(8 * g, 8 * g + 8)
                for m in range(2):
                    turn = lax.rem(255 - (64 * m + 4 * x + g), 128)
                    for q, ref in enumerate((stiffs, mass_terms)):
                        ref[m, x, rows, :] = jnp.where(
                            last, pltpu.roll(edge[q], turn, 1), ref[m, x, rows, :]
                        )
        return 0

    lax.fori_loop(0, 4, patch_last, 0)

    top_t = math.tanh(4.0)
    merge_z(0, z_waits[0])
    eigs = [eig[m] for m in range(2)]

    def project(xb, acc):
        acc = list(acc)
        for i in range(4):
            x = 4 * xb + i
            xpos = mx * TX + x
            x1 = inside(xpos - 1, cx * TX) + inside(xpos + 1, cx * TX)
            x2 = inside(xpos - 2, cx * TX) + inside(xpos + 2, cx * TX)
            for g in range(4):
                rows = slice(8 * g, 8 * g + 8)
                inverse = 1.0 / (wparts[0, g] + x1 * wparts[1, g] + x2 * wparts[2, g])
                t = jnp.tanh(8.0 * ((fz[x, rows, :] + from_z(0, xb, i, g)) * inverse - 0.5))
                rho = (top_t + t) * (0.5 / top_t)
                slopes[x, rows, :] = (1.0 - t * t) * inverse * (4.0 / top_t)
                cubics[x, rows, :] = (3.0 * (1.0 - 0.001)) * (rho * rho)
                for m in range(2):
                    acc[m] = acc[m] + rho * mass_terms[m, x, rows, :]
        return tuple(acc)

    masses = lax.fori_loop(0, 4, project, (zero, zero))
    for m in range(2):
        a_in[a_slot, m : m + 1, :] = jnp.sum(masses[m], axis=0, keepdims=True)

    def spread_sum(ref, count, slot, device, sem):
        def start(k, _):
            @pl.when(k != slot)
            def _():
                remote(ref.at[slot], ref.at[slot], sem, device(k)).start()

            return 0

        for k in range(count):
            start(k, 0)
        return remote(ref.at[pl.ds(0, count - 1)], ref.at[pl.ds(0, count - 1)], sem, me)

    a_copies = spread_sum(a_in, a_count, a_slot, a_device, 29)

    def gradients(xb, _):
        for i in range(4):
            for g in range(4):
                x, rows = 4 * xb + i, slice(8 * g, 8 * g + 8)
                for m in range(2):
                    gp[m, x + 2, 8 + 8 * g : 16 + 8 * g, :] = (
                        cubics[x, rows, :] * stiffs[m, x, rows, :]
                        - eigs[m] * mass_terms[m, x, rows, :]
                    ) * slopes[x, rows, :]
        return 0

    lax.fori_loop(0, 4, gradients, 0)
    flats = send_flats(gp, gp, (slice(None),), (2, 8), 15)

    for wait in flats:
        wait()
    clear_halo(gp, (slice(None),))
    stores = []
    for m in range(2):

        def put_grad(x, g, value, m=m):
            outs[m, x, 8 * g : 8 * g + 8, :] = value

        sweep(lambda p, a, b, m=m: gp[m, p, a:b, :], put_grad, z_out.at[1 + m])
        z_waits.append(send_z(1 + m))
        if m == 0:
            a_copies.wait_recv()
            b_in[b_slot] = jnp.sum(a_in[...], axis=0)
            b_copies = spread_sum(b_in, b_count, b_slot, b_device, 30)

    for m in range(2):
        merge_z(1 + m, z_waits[1 + m])

        def finish(xb, _, m=m):
            for i in range(4):
                for g in range(4):
                    rows = slice(8 * g, 8 * g + 8)
                    outs[m, 4 * xb + i, rows, :] = outs[m, 4 * xb + i, rows, :] + from_z(
                        1 + m, xb, i, g
                    )
            return 0

        lax.fori_loop(0, 4, finish, 0)
        store = pltpu.make_async_copy(outs.at[m], raw_ref.at[m], out_sem.at[m])
        store.start()
        stores.append(store)

    for wait in sent:
        wait()
    a_copies.wait_send()
    for store in stores:
        store.wait()
    b_copies.wait_recv()
    total = jnp.sum(jnp.sum(b_in[...], axis=0), axis=1, keepdims=True)
    scale_ref[...] = jnp.broadcast_to(count / total, (2, 128))
    b_copies.wait_send()


def per_device(sizes, design, modes, eigenvalues):
    cx, cy, cz = sizes
    a_count, b_count = (cx // 2) * cz, 2 * cy
    dma = pltpu.SemaphoreType.DMA

    def vmem(*shape):
        return pltpu.VMEM(shape, F32)

    arguments = (design, modes.reshape(6, TX, TY, TZ), eigenvalues)
    raw, scale = pl.pallas_call(
        lambda *refs: kernel(sizes, *refs),
        out_shape=(
            jax.ShapeDtypeStruct((2, TX, TY, TZ), F32),
            jax.ShapeDtypeStruct((2, 128), F32),
        ),
        in_specs=[pl.BlockSpec(memory_space=pl.ANY)] * 3,
        out_specs=(
            pl.BlockSpec(memory_space=pl.ANY),
            pl.BlockSpec(memory_space=pltpu.VMEM),
        ),
        scratch_shapes=[
            vmem(TX + 4, TY + 16, TZ),
            vmem(6, TX + 1, TY + 8, TZ),
            vmem(6, TX + 1, TY + 8, TZ),
            vmem(2, 3, 8, 128),
            vmem(4, 3, 8, 128),
            vmem(4, 3, 8, 128),
            vmem(2, 8, 128),
            vmem(3, 4, 8, 128),
            vmem(TX, TY, TZ),
            vmem(TX, TY, TZ),
            vmem(TX, TY, TZ),
            vmem(2, TX, TY, TZ),
            vmem(2, TX, TY, TZ),
            vmem(2, TX + 4, TY + 16, TZ),
            vmem(2, TX, TY, TZ),
            vmem(3, 2, 8, 128),
            vmem(3, 2, 8, 128),
            vmem(3, 2, 8, 128),
            vmem(a_count, 2, 128),
            vmem(b_count, 2, 128),
            pltpu.SMEM((2,), F32),
            dma((8,)),
            dma((2,)),
            dma((34,)),
            dma((34,)),
        ],
        compiler_params=pltpu.CompilerParams(
            collective_id=0, has_side_effects=True, vmem_limit_bytes=24 * 1024 * 1024
        ),
    )(*(pltpu.with_memory_space_constraint(v, pltpu.HBM) for v in arguments))
    return raw * scale[:, None, None, :]


def solution(mesh):
    sizes = tuple(mesh.shape[a] for a in AXES)
    return jax.shard_map(
        lambda design, modes, eigenvalues: per_device(sizes, design, modes, eigenvalues),
        mesh=mesh,
        in_specs=(P("gx", "gy", "gz"), P(None, None, "gx", "gy", "gz"), P()),
        out_specs=P(None, "gx", "gy", "gz"),
        check_vma=False,
    )
```

```python
import functools
import itertools
import math

import jax
import jax.numpy as jnp
from jax import lax
from jax.experimental import pallas as pl
from jax.experimental.pallas import tpu as pltpu
from jax.sharding import PartitionSpec as P

AXES = ("gx", "gy", "gz")
MESH = pl.DeviceIdType.MESH
TX, TY, TZ = 16, 32, 128
FLAT = [o for o in itertools.product((-1, 0, 1), (-1, 0, 1), (0,)) if o != (0, 0, 0)]
SIDES = [(-1, 0, 0), (0, -1, 0), (-1, -1, 0)]
BELOW = [(0, 0, -1), (0, -1, -1), (-1, 0, -1), (-1, -1, -1)]
F32 = jnp.float32


def weight(i, j, k):
    return max(0.0, 3.0 - math.sqrt(i * i + j * j + k * k))


X_SPAN = {-1: (0, TX + 2, 2), 0: (0, 2, TX), 1: (TX - 2, 0, 2)}
Y_SPAN = {-1: (0, TY + 8, 2), 0: (0, 8, TY), 1: (TY - 2, 6, 2)}


def combine(values, weights):
    total = None
    for value, w in zip(values, weights):
        if w == 0.0:
            continue
        total = w * value if total is None else total + w * value
    return total


def loop(n, body, init, by=1):
    def block(q, carry):
        for i in range(by):
            carry = body(q * by + i, carry)
        return carry

    return block(0, init) if by == n else lax.fori_loop(0, n // by, block, init)


def kernel(
    sizes,
    design_ref,
    modes_ref,
    eig_ref,
    raw_ref,
    scale_ref,
    dp,
    mb,
    mz,
    face,
    from_hi,
    from_side,
    edge,
    wparts,
    fz,
    slopes,
    cubics,
    stiffs,
    mass_terms,
    gp,
    outs,
    z_out,
    z_up,
    z_down,
    a_in,
    b_in,
    eig,
    local_sem,
    out_sem,
    send_sem,
    recv_sem,
):
    cx, cy, cz = sizes
    count = float(cx * TX * cy * TY * cz * TZ)
    me = tuple(lax.axis_index(a) for a in AXES)
    mx, my, mzi = me

    def near(o):
        return tuple(m + d if d else m for m, d in zip(me, o))

    def there(o):
        ok = None
        for m, d, size in zip(me, o, sizes):
            if d:
                here = m > 0 if d < 0 else m < size - 1
                ok = here if ok is None else ok & here
        return ok

    def opposite(o):
        return tuple(-d for d in o)

    a_count, b_count = (cx // 2) * cz, 2 * cy
    a_slot = (mx // 2) * cz + mzi
    b_slot = lax.rem(mx, 2) * cy + my

    def a_device(slot):
        return ((slot // cz) * 2 + lax.rem(mx, 2), my, lax.rem(slot, cz))

    def b_device(slot):
        return ((mx // 2) * 2 + slot // cy, lax.rem(slot, cy), mzi)

    barrier = pltpu.get_barrier_semaphore()

    def greet(device):
        pl.semaphore_signal(barrier, inc=1, device_id=device, device_id_type=MESH)

    def greet_a(k, _):
        greet(a_device(lax.rem(a_slot + k, a_count)))
        return 0

    def greet_b(k, _):
        greet(b_device(lax.rem(b_slot + k, b_count)))
        return 0

    for k in range(1, a_count):
        greet_a(k, 0)
    for k in range(1, b_count):
        greet_b(k, 0)

    heard = a_count - 1 + b_count - 1
    for o in FLAT + [(0, 0, 1), (0, 0, -1)] + BELOW[1:]:
        heard = heard + there(o).astype(jnp.int32)
    for o in FLAT + [(0, 0, 1), (0, 0, -1)] + [opposite(o) for o in BELOW[1:]]:

        @pl.when(there(o))
        def _(o=o):
            greet(near(o))

    loads = [
        pltpu.make_async_copy(design_ref, dp.at[pl.ds(2, TX), pl.ds(8, TY)], local_sem.at[0])
    ]
    for c in range(6):
        loads.append(
            pltpu.make_async_copy(
                modes_ref.at[c], mb.at[c, pl.ds(0, TX), pl.ds(0, TY)], local_sem.at[1 + c]
            )
        )
    loads.append(pltpu.make_async_copy(eig_ref, eig, local_sem.at[7]))
    for load in loads:
        load.start()

    lane = lax.broadcasted_iota(jnp.int32, (8, 128), 1)
    quad = lax.shift_right_logical(lax.rem(lane + 2, 128), 2)
    first_two, last_two = lane < 2, lane >= 126
    zero = jnp.zeros((8, 128), F32)

    pl.semaphore_wait(barrier, heard)

    sent = []

    def remote(src, dst, sem, device):
        return pltpu.make_async_remote_copy(
            src_ref=src,
            dst_ref=dst,
            send_sem=send_sem.at[sem],
            recv_sem=recv_sem.at[sem],
            device_id=device,
            device_id_type=MESH,
        )

    def send(o, src, dst, sem):
        @pl.when(there(o))
        def _():
            remote(src, dst, sem, near(o)).start()

        def sent_all():
            @pl.when(there(o))
            def _():
                remote(src, dst, sem, near(o)).wait_send()

        def received():
            @pl.when(there(opposite(o)))
            def _():
                remote(src, dst, sem, near(o)).wait_recv()

        sent.append(sent_all)
        return received

    def send_flats(src, dst, lead, shift, sem):
        waits = []
        for i, o in enumerate(FLAT):
            (xs, xd, xn), (ys, yd, yn) = X_SPAN[o[0]], Y_SPAN[o[1]]
            waits.append(
                send(
                    o,
                    src.at[lead + (pl.ds(xs + shift[0], xn), pl.ds(ys + shift[1], yn))],
                    dst.at[lead + (pl.ds(xd, xn), pl.ds(yd, yn))],
                    sem + i,
                )
            )
        return waits

    loads[0].wait()
    design_waits = send_flats(dp, dp, (), (2, 8), 0)
    mode_waits = []
    for i, o in enumerate(SIDES):
        dx, dy, _ = o
        xs = pl.ds(0, 1) if dx else pl.ds(0, TX)
        xd = pl.ds(TX, 1) if dx else pl.ds(0, TX)
        ys = pl.ds(0, 1) if dy else pl.ds(0, TY)
        yd = pl.ds(TY, 1) if dy else pl.ds(0, TY)
        mode_waits.append(send(o, modes_ref.at[:, xs, ys], mb.at[:, xd, yd], 8 + i))

    def inside(cell, total):
        return ((cell >= 0) & (cell < total)).astype(F32)

    zpos = mzi * TZ + lane
    z1 = inside(zpos - 1, cz * TZ) + inside(zpos + 1, cz * TZ)
    z2 = inside(zpos - 2, cz * TZ) + inside(zpos + 2, cz * TZ)
    for g in range(4):
        ypos = my * TY + 8 * g + lax.broadcasted_iota(jnp.int32, (8, 128), 0)
        y1 = inside(ypos - 1, cy * TY) + inside(ypos + 1, cy * TY)
        y2 = inside(ypos - 2, cy * TY) + inside(ypos + 2, cy * TY)
        for i in range(3):
            rows = [
                weight(i, j, 0) + weight(i, j, 1) * z1 + weight(i, j, 2) * z2 for j in range(3)
            ]
            wparts[i, g] = rows[0] + y1 * rows[1] + y2 * rows[2]

    for load in loads[1:]:
        load.wait()

    def pack_modes(x, carry):
        first, final = (list(v) for v in carry)
        for c in range(6):
            for g in range(4):
                k = (c // 3) * 64 + 4 * x + g
                r = pltpu.roll(mb[c, x, 8 * g : 8 * g + 8, :], k, 1)
                first[c % 3] = jnp.where(lane == k, r, first[c % 3])
                final[c % 3] = jnp.where(lane == (k + 127) % 128, r, final[c % 3])
        return tuple(first), tuple(final)

    first, final = loop(TX, pack_modes, ((zero,) * 3, (zero,) * 3), TX)
    for c in range(3):
        face[0, c] = first[c]
        face[1, c] = pltpu.roll(final[c], 1, 1)

    face_waits = []
    for i, o in enumerate(BELOW):
        face_waits.append(send(o, face.at[0], from_hi.at[-2 * o[0] - o[1]], 11 + i))
    for i, o in enumerate(SIDES):
        face_waits.append(send(o, face.at[1], from_side.at[-2 * o[0] - o[1]], 31 + i))

    def shift_modes(x, _):
        for c in range(6):
            for g in range(4):
                rows = slice(8 * g, 8 * g + 8)
                mz[c, x, rows, :] = pltpu.roll(mb[c, x, rows, :], 127, 1)
        return 0

    loop(TX, shift_modes, 0, 4)

    def clear(ref, index, cond):
        @pl.when(cond)
        def _():
            ref[index] = jnp.zeros_like(ref[index])

    def clear_halo(ref, lead):
        clear(ref, lead + (slice(0, 2),), mx == 0)
        clear(ref, lead + (slice(TX + 2, TX + 4),), mx == cx - 1)
        clear(ref, lead + (slice(None), slice(0, 8)), my == 0)
        clear(ref, lead + (slice(None), slice(TY + 8, TY + 16)), my == cy - 1)

    order = ((0, 0), (0, 1), (1, 1), (0, 2), (1, 2), (2, 2))

    def sweep(load, put, packs):
        packs[0] = zero
        packs[1] = zero

        def body(xb, _):
            held = packs[xb // 2]
            for g in range(4):
                top = 8 + 8 * g
                a = {}
                for t in range(8):
                    p = 4 * xb + t
                    a[t, 0] = load(p, top, top + 8)
                    a[t, 1] = load(p, top - 1, top + 7) + load(p, top + 1, top + 9)
                    a[t, 2] = load(p, top - 2, top + 6) + load(p, top + 2, top + 10)
                for i in range(4):
                    b = {}
                    for j in range(3):
                        b[0, j] = a[i + 2, j]
                        b[1, j] = a[i + 1, j] + a[i + 3, j]
                        b[2, j] = a[i, j] + a[i + 4, j]
                    grouped = [b[u, v] if u == v else b[u, v] + b[v, u] for u, v in order]
                    e0, e1, e2 = (
                        combine(grouped, [weight(u, v, k) for u, v in order]) for k in range(3)
                    )
                    up, down = pltpu.roll(e1, 1, 1), pltpu.roll(e1, 127, 1)
                    up2, down2 = pltpu.roll(e2, 2, 1), pltpu.roll(e2, 126, 1)
                    out = jnp.where(lane < 1, up, jnp.where(lane >= 127, down, 0.0)) + jnp.where(
                        first_two, up2, jnp.where(last_two, down2, 0.0)
                    )
                    put(4 * xb + i, g, (e0 + ((up + down) + (up2 + down2))) - out)
                    k = lax.rem(xb, 2) * 16 + 4 * i + g
                    held = jnp.where(quad == k, pltpu.roll(out, 4 * k, 1), held)
            packs[xb // 2] = held
            return 0

        lax.fori_loop(0, 4, body, 0)

    def send_z(f):
        return (
            send((0, 0, -1), z_out.at[f], z_up.at[f], 23 + f),
            send((0, 0, 1), z_out.at[f], z_down.at[f], 26 + f),
        )

    def merge_z(f, waits):
        for wait in waits:
            wait()
        clear(z_up, f, mzi == cz - 1)
        clear(z_down, f, mzi == 0)
        for h in range(2):
            z_up[f, h] = jnp.where(lax.rem(lane, 4) >= 2, z_up[f, h], z_down[f, h])

    def from_z(f, xb, i, g):
        k = lax.rem(xb, 2) * 16 + 4 * i + g
        r = pltpu.roll(z_up[f, xb // 2], lax.rem(128 - 4 * k, 128), 1)
        return jnp.where(first_two | last_two, r, 0.0)

    factor = 1.0 / (1.3 * 0.4)
    lam, mu = 0.3 * factor, 0.2 * factor

    def across(v0, v1, w0, w1):
        vs, vd, ws, wd = v0 + v1, v1 - v0, w0 + w1, w1 - w0
        return vs + ws, ws - vs, vd + wd, wd - vd

    def plane(c, x, g):
        a, b = 8 * g, 8 * g + 8
        v0, v1 = mb[c, x, a:b, :], mb[c, x, a + 1 : b + 1, :]
        return across(v0, v1, mz[c, x, a:b, :], mz[c, x, a + 1 : b + 1, :])

    def energies(now, later):
        a = {}
        for c in range(3):
            for q, (j, k) in enumerate(((0, 0), (0, 1), (1, 0), (1, 1))):
                a[c, 0, j, k] = now[4 * c + q] + later[4 * c + q]
                a[c, 1, j, k] = later[4 * c + q] - now[4 * c + q]
        s = {key: v * v for key, v in a.items()}

        def sq(v):
            return v * v

        q0 = s[0, 0, 0, 0] + s[1, 0, 0, 0] + s[2, 0, 0, 0]
        axial = s[0, 1, 0, 0] + s[1, 0, 1, 0] + s[2, 0, 0, 1]
        slide = (
            (s[0, 0, 1, 0] + s[0, 0, 0, 1])
            + (s[1, 1, 0, 0] + s[1, 0, 0, 1])
            + (s[2, 1, 0, 0] + s[2, 0, 1, 0])
        )
        q1 = axial + slide
        bend = (
            (s[0, 1, 1, 0] + s[0, 1, 0, 1])
            + (s[1, 1, 1, 0] + s[1, 0, 1, 1])
            + (s[2, 1, 0, 1] + s[2, 0, 1, 1])
        )
        twist = s[0, 0, 1, 1] + s[1, 1, 0, 1] + s[2, 1, 1, 0]
        q2 = bend + twist
        q3 = s[0, 1, 1, 1] + s[1, 1, 1, 1] + s[2, 1, 1, 1]
        mass = (1 / 64) * q0 + (1 / 192) * q1 + ((1 / 576) * q2 + (1 / 1728) * q3)
        trace = sq(a[0, 1, 0, 0] + a[1, 0, 1, 0] + a[2, 0, 0, 1])
        cross = (
            a[0, 0, 1, 0] * a[1, 1, 0, 0]
            + a[1, 0, 0, 1] * a[2, 0, 1, 0]
            + a[0, 0, 0, 1] * a[2, 1, 0, 0]
        )
        cross_1 = (
            a[0, 1, 1, 0] * a[2, 0, 1, 1]
            + a[0, 1, 0, 1] * a[1, 0, 1, 1]
            + a[1, 1, 1, 0] * a[2, 1, 0, 1]
        )
        shear_1 = sq(a[0, 0, 1, 1] + a[1, 1, 0, 1] + a[2, 1, 1, 0]) + twist
        stiff = (
            ((lam / 16) * trace + (mu / 8) * (axial + cross))
            + ((mu / 16) * slide + (lam / 24) * cross_1)
            + ((mu / 16 + lam / 48) * bend + (mu / 48) * shear_1)
            + ((lam + 4 * mu) / 144) * q3
        )
        return stiff, mass

    def element_pass(spans, m, _):
        for pairs, x_from, x_to in spans:
            groups = (2 * pairs, 2 * pairs + 1)

            def body(x, held):
                nexts = []
                for i, g in enumerate(groups):
                    later = sum((plane(3 * m + c, x + 1, g) for c in range(3)), ())
                    nexts += later
                    stiff, mass = energies(held[12 * i : 12 * i + 12], later)
                    stiffs[m, x, 8 * g : 8 * g + 8, :] = stiff
                    mass_terms[m, x, 8 * g : 8 * g + 8, :] = mass
                return tuple(nexts)

            first = []
            for g in groups:
                first += sum((plane(3 * m + c, x_from, g) for c in range(3)), ())
            lax.fori_loop(x_from, x_to, body, tuple(first))
        return 0

    lax.fori_loop(0, 2, functools.partial(element_pass, ((0, 0, TX - 1),)), 0)

    for wait in design_waits:
        wait()
    clear_halo(dp, ())

    def put_design(x, g, value):
        fz[x, 8 * g : 8 * g + 8, :] = value

    sweep(lambda p, a, b: dp[p, a:b, :], put_design, z_out.at[0])
    z_waits = [send_z(0)]

    for wait in mode_waits:
        wait()
    clear(mb, (slice(None), TX), mx == cx - 1)
    clear(mb, (slice(None), slice(None), slice(TY, TY + 8)), my == cy - 1)

    def shift_halo(c, _):
        for x in range(TX + 1):
            mz[c, x, TY : TY + 8, :] = pltpu.roll(mb[c, x, TY : TY + 8, :], 127, 1)
        for g in range(4):
            rows = slice(8 * g, 8 * g + 8)
            mz[c, TX, rows, :] = pltpu.roll(mb[c, TX, rows, :], 127, 1)
        return 0

    loop(6, shift_halo, 0, 2)

    lax.fori_loop(0, 2, functools.partial(element_pass, ((0, TX - 1, TX), (1, 0, TX))), 0)

    for wait in face_waits:
        wait()
    for o in BELOW:
        clear(from_hi, -2 * o[0] - o[1], jnp.logical_not(there(opposite(o))))
    for o in SIDES:
        clear(from_side, -2 * o[0] - o[1], jnp.logical_not(there(opposite(o))))
    below_last = lax.broadcasted_iota(jnp.int32, (8, 128), 0) < 7
    last_group, last_plane = lax.rem(lane, 4) == 3, lax.rem(lane, 64) >= 60

    def next_y(own, halo):
        own, halo = pltpu.roll(own, 7, 0), pltpu.roll(halo, 7, 0)
        over = jnp.where(last_group, pltpu.roll(halo, 3, 1), pltpu.roll(own, 127, 1))
        return jnp.where(below_last, own, over)

    def next_x(own, halo):
        return jnp.where(last_plane, pltpu.roll(halo, 60, 1), pltpu.roll(own, 124, 1))

    now, later = (), ()
    for c in range(3):
        sides = []
        for own, side in ((face[1, c], from_side), (from_hi[0, c], from_hi)):
            own_y, x_halo = next_y(own, side[1, c]), side[2, c]
            x_halo_y = next_y(x_halo, side[3, c])
            sides.append((own, own_y, next_x(own, x_halo), next_x(own_y, x_halo_y)))
        (v00, v01, v10, v11), (w00, w01, w10, w11) = sides
        now += across(v00, v01, w00, w01)
        later += across(v10, v11, w10, w11)
    edge[0], edge[1] = energies(now, later)
    last = lane >= 127

    def patch_last(xb, _):
        for i in range(4):
            for g in range(4):
                x, rows = 4 * xb + i, slice(8 * g, 8 * g + 8)
                for m in range(2):
                    turn = lax.rem(255 - (64 * m + 4 * x + g), 128)
                    for q, ref in enumerate((stiffs, mass_terms)):
                        ref[m, x, rows, :] = jnp.where(
                            last, pltpu.roll(edge[q], turn, 1), ref[m, x, rows, :]
                        )
        return 0

    lax.fori_loop(0, 4, patch_last, 0)

    top_t = math.tanh(4.0)
    merge_z(0, z_waits[0])
    eigs = [eig[m] for m in range(2)]

    def project(xb, acc):
        acc = list(acc)
        for i in range(4):
            x = 4 * xb + i
            xpos = mx * TX + x
            x1 = inside(xpos - 1, cx * TX) + inside(xpos + 1, cx * TX)
            x2 = inside(xpos - 2, cx * TX) + inside(xpos + 2, cx * TX)
            for g in range(4):
                rows = slice(8 * g, 8 * g + 8)
                inverse = 1.0 / (wparts[0, g] + x1 * wparts[1, g] + x2 * wparts[2, g])
                t = jnp.tanh(8.0 * ((fz[x, rows, :] + from_z(0, xb, i, g)) * inverse - 0.5))
                rho = (top_t + t) * (0.5 / top_t)
                slopes[x, rows, :] = (1.0 - t * t) * inverse * (4.0 / top_t)
                cubics[x, rows, :] = (3.0 * (1.0 - 0.001)) * (rho * rho)
                for m in range(2):
                    acc[m] = acc[m] + rho * mass_terms[m, x, rows, :]
        return tuple(acc)

    masses = lax.fori_loop(0, 4, project, (zero, zero))
    for m in range(2):
        b_in[b_slot, m : m + 1, :] = jnp.sum(masses[m], axis=0, keepdims=True)

    def spread_sum(ref, count, slot, device, sem):
        def start(k, _):
            @pl.when(k != slot)
            def _():
                remote(ref.at[slot], ref.at[slot], sem, device(k)).start()

            return 0

        for k in range(count):
            start(k, 0)
        return remote(ref.at[pl.ds(0, count - 1)], ref.at[pl.ds(0, count - 1)], sem, me)

    b_copies = spread_sum(b_in, b_count, b_slot, b_device, 30)

    def gradients(xb, _):
        for i in range(4):
            for g in range(4):
                x, rows = 4 * xb + i, slice(8 * g, 8 * g + 8)
                for m in range(2):
                    gp[m, x + 2, 8 + 8 * g : 16 + 8 * g, :] = (
                        cubics[x, rows, :] * stiffs[m, x, rows, :]
                        - eigs[m] * mass_terms[m, x, rows, :]
                    ) * slopes[x, rows, :]
        return 0

    lax.fori_loop(0, 4, gradients, 0)
    flats = send_flats(gp, gp, (slice(None),), (2, 8), 15)

    for wait in flats:
        wait()
    clear_halo(gp, (slice(None),))
    stores = []
    for m in range(2):

        def put_grad(x, g, value, m=m):
            outs[m, x, 8 * g : 8 * g + 8, :] = value

        sweep(lambda p, a, b, m=m: gp[m, p, a:b, :], put_grad, z_out.at[1 + m])
        z_waits.append(send_z(1 + m))
        if m == 0:
            b_copies.wait_recv()
            a_in[a_slot] = jnp.sum(b_in[...], axis=0)
            a_copies = spread_sum(a_in, a_count, a_slot, a_device, 29)

    for m in range(2):
        merge_z(1 + m, z_waits[1 + m])

        def finish(xb, _, m=m):
            for i in range(4):
                for g in range(4):
                    rows = slice(8 * g, 8 * g + 8)
                    outs[m, 4 * xb + i, rows, :] = outs[m, 4 * xb + i, rows, :] + from_z(
                        1 + m, xb, i, g
                    )
            return 0

        lax.fori_loop(0, 4, finish, 0)
        store = pltpu.make_async_copy(outs.at[m], raw_ref.at[m], out_sem.at[m])
        store.start()
        stores.append(store)

    for wait in sent:
        wait()
    b_copies.wait_send()
    for store in stores:
        store.wait()
    a_copies.wait_recv()
    total = jnp.sum(jnp.sum(a_in[...], axis=0), axis=1, keepdims=True)
    scale_ref[...] = jnp.broadcast_to(count / total, (2, 128))
    a_copies.wait_send()


def per_device(sizes, design, modes, eigenvalues):
    cx, cy, cz = sizes
    a_count, b_count = (cx // 2) * cz, 2 * cy
    dma = pltpu.SemaphoreType.DMA

    def vmem(*shape):
        return pltpu.VMEM(shape, F32)

    arguments = (design, modes.reshape(6, TX, TY, TZ), eigenvalues)
    raw, scale = pl.pallas_call(
        lambda *refs: kernel(sizes, *refs),
        out_shape=(
            jax.ShapeDtypeStruct((2, TX, TY, TZ), F32),
            jax.ShapeDtypeStruct((2, 128), F32),
        ),
        in_specs=[pl.BlockSpec(memory_space=pl.ANY)] * 3,
        out_specs=(
            pl.BlockSpec(memory_space=pl.ANY),
            pl.BlockSpec(memory_space=pltpu.VMEM),
        ),
        scratch_shapes=[
            vmem(TX + 4, TY + 16, TZ),
            vmem(6, TX + 1, TY + 8, TZ),
            vmem(6, TX + 1, TY + 8, TZ),
            vmem(2, 3, 8, 128),
            vmem(4, 3, 8, 128),
            vmem(4, 3, 8, 128),
            vmem(2, 8, 128),
            vmem(3, 4, 8, 128),
            vmem(TX, TY, TZ),
            vmem(TX, TY, TZ),
            vmem(TX, TY, TZ),
            vmem(2, TX, TY, TZ),
            vmem(2, TX, TY, TZ),
            vmem(2, TX + 4, TY + 16, TZ),
            vmem(2, TX, TY, TZ),
            vmem(3, 2, 8, 128),
            vmem(3, 2, 8, 128),
            vmem(3, 2, 8, 128),
            vmem(a_count, 2, 128),
            vmem(b_count, 2, 128),
            pltpu.SMEM((2,), F32),
            dma((8,)),
            dma((2,)),
            dma((34,)),
            dma((34,)),
        ],
        compiler_params=pltpu.CompilerParams(
            collective_id=0, has_side_effects=True, vmem_limit_bytes=24 * 1024 * 1024
        ),
    )(*(pltpu.with_memory_space_constraint(v, pltpu.HBM) for v in arguments))
    return raw * scale[:, None, None, :]


def solution(mesh):
    sizes = tuple(mesh.shape[a] for a in AXES)
    return jax.shard_map(
        lambda design, modes, eigenvalues: per_device(sizes, design, modes, eigenvalues),
        mesh=mesh,
        in_specs=(P("gx", "gy", "gz"), P(None, None, "gx", "gy", "gz"), P()),
        out_specs=P(None, "gx", "gy", "gz"),
        check_vma=False,
    )
```
